256 devices in a mesh: seq: 32 (over x, z), chan: 8 (over y, core).
Axes of the slice: x: 4, y: 4, z: 8, core: 2. Of those that a mesh axis runs over, the one named last changes fastest.
Arguments:
- projections: bfloat16 [3, 8192, 4096], P(None, 'seq', 'chan'), may hold values from -6 to 6
- short_taps: float32 [3, 7, 4096], P(None, None, 'chan'), may hold values from -2 to 2
- filters: float32 [16, 8192], P('chan', 'seq'), may hold values from -0.0625 to 0.0625
- out_weight: bfloat16 [4096, 4096], P(None, 'chan'), may hold values from -0.09375 to 0.09375
Outputs:
- layer_output: bfloat16 [8192, 4096], P('seq', 'chan')
The draws below stay inside these ranges and needn't reach their ends.
All inputs are finite; a program needn't handle non-finite values.
Results may differ from the reference program's by a relative error of at most 0.0049.
Values may be sent and summed in bfloat16 or wider, within the bound.
A program may use at most 64 MiB of HBM per device.

```python
import jax
import jax.numpy as jnp
from jax import lax

D = 4096
GROUP = 256
TAPS = 7
L = 8192
G = 16


def block_levels(key, extent, shards, low, top_value):
    level = 1.0
    for axis_at, parts in shards:
        heights = jax.random.uniform(jax.random.fold_in(jax.random.fold_in(key, 6), axis_at), (parts,), jnp.float32, low / len(shards), top_value / len(shards))
        level = level * jnp.repeat(jnp.exp(heights), extent[axis_at] // parts).reshape((-1,) + (1,) * (len(extent) - 1 - axis_at))
    return level


def gaussian(rng, dims, width, bound, pieces=(), kind=jnp.bfloat16):
    array = jax.random.normal(rng, dims, jnp.float32) * width
    if len(pieces) > 0:
        array = block_levels(rng, dims, pieces, -0.22, 0.18) * array
    return jnp.clip(array, min=-bound, max=bound).astype(kind)


def setup_inputs(seed: int = 0) -> dict:
    key_of = jax.random.split(jax.random.key(seed), 5)
    return {
        "projections": gaussian(key_of[0], (3, L, D), 1.0, 6.0, ((1, 32), (2, 8))),
        "short_taps": gaussian(key_of[1], (3, TAPS, D), TAPS ** -0.5, 2.0, ((2, 8),), jnp.float32),
        "filters": gaussian(key_of[2], (G, L), L ** -0.5, 0.0625, ((0, 8), (1, 32)), jnp.float32),
        "out_weight": gaussian(key_of[3], (D, D), D ** -0.5, 0.09375, ((1, 8),)),
    }


def reference(projections, short_taps, filters, out_weight):
    length = projections.shape[1]

    def one_group(group_index):
        first_column = group_index * GROUP
        projected = lax.dynamic_slice_in_dim(projections, first_column, GROUP, 2).astype(jnp.float32)
        weights = lax.dynamic_slice_in_dim(short_taps, first_column, GROUP, 2)
        padded = jnp.pad(projected, ((0, 0), (TAPS - 1, 0), (0, 0)))
        filtered = jnp.zeros(projected.shape, jnp.float32)
        for tap_index in range(TAPS):
            filtered = filtered + weights[:, tap_index, None, :] * padded[:, TAPS - 1 - tap_index:TAPS - 1 - tap_index + length, :]
        product = filtered[1] * filtered[2]
        kernel = lax.dynamic_slice_in_dim(filters, group_index, 1, 0)[0]
        padded_size = 2 * length
        spectrum = jnp.fft.rfft(product, n=padded_size, axis=0) * jnp.fft.rfft(kernel, n=padded_size)[:, None]
        long_part = jnp.fft.irfft(spectrum, n=padded_size, axis=0)[:length]
        return (filtered[0] * long_part).astype(jnp.bfloat16)

    gated_rows = lax.map(one_group, jnp.arange(G, dtype=jnp.int32))
    gated_rows = jnp.transpose(gated_rows, (1, 0, 2)).reshape(length, D)
    return jnp.dot(gated_rows, out_weight, preferred_element_type=jnp.float32).astype(jnp.bfloat16)
```

```python
import functools

import jax
import jax.numpy as jnp
from jax import lax
from jax.experimental import pallas as pl
from jax.experimental.pallas import tpu as pltpu
from jax.sharding import PartitionSpec as P

MESH = pl.DeviceIdType.MESH
TAPS = 7
PAD = 16
LANES = 128


def kernel(
    sizes,
    proj_hbm,
    taps_ref,
    filt_ref,
    weight_hbm,
    out_ref,
    proj,
    halo,
    ext,
    filt_all,
    high,
    low,
    product_out,
    product_in,
    total,
    conv_out,
    conv_in,
    query,
    gated,
    weight,
    out_total,
    load_sem,
    self_sem,
    halo_sem,
    filt_sem,
    product_sem,
    conv_send,
    conv_recv,
    gated_send,
    gated_recv,
):
    count, planes, rings = sizes
    rows = proj.shape[1]
    channels = proj.shape[2]
    share = channels // count
    blocks = channels // LANES
    per_block = count // blocks
    me = lax.axis_index("seq")
    chan = lax.axis_index("chan")
    x, z = me // rings, lax.rem(me, rings)
    y, core = chan // 2, lax.rem(chan, 2)
    heights = lax.axis_size("chan") // 2
    step_up = 1 - 2 * core
    down = lax.rem(y + step_up + heights, heights) * 2 + core
    up = lax.rem(y - step_up + heights, heights) * 2 + core
    far = lax.rem(y + 2, heights) * 2 + core
    sibling = y * 2 + 1 - core
    following = lax.rem(me + 1, count)
    group_of = me // (count // filt_ref.shape[0])

    load = pltpu.make_async_copy(proj_hbm, proj, load_sem.at[0])
    load.start()
    load_weight = pltpu.make_async_copy(weight_hbm, weight, load_sem.at[1])
    load_weight.start()

    barrier = pltpu.get_barrier_semaphore()

    def peer(k):
        px = lax.rem(x + k // rings, planes)
        pz = lax.rem(z + lax.rem(k, rings), rings)
        return px * rings + pz

    def greet(k, carry):
        pl.semaphore_signal(barrier, inc=1, device_id={"seq": peer(k)}, device_id_type=MESH)
        return carry

    lax.fori_loop(1, count, greet, 0)
    for other in (down, up, sibling):
        pl.semaphore_signal(barrier, inc=1, device_id={"chan": other}, device_id_type=MESH)
    pl.semaphore_wait(barrier, count + 2)

    halo_copy = pltpu.make_async_remote_copy(
        src_ref=proj_hbm.at[:, pl.ds(rows - PAD, PAD), :],
        dst_ref=halo,
        send_sem=halo_sem.at[0],
        recv_sem=halo_sem.at[1],
        device_id={"seq": following},
        device_id_type=MESH,
    )
    halo_copy.start()

    def send_filter(k, carry):
        pltpu.make_async_remote_copy(
            src_ref=filt_ref,
            dst_ref=filt_all.at[me + 1],
            send_sem=filt_sem.at[0],
            recv_sem=filt_sem.at[1],
            device_id={"seq": peer(k)},
            device_id_type=MESH,
        ).start()
        return carry

    lax.fori_loop(1, count, send_filter, 0)
    pltpu.make_async_copy(filt_ref, filt_all.at[me + 1], filt_sem.at[1]).start()
    filt_all[0] = jnp.zeros(filt_all.shape[1:], jnp.float32)

    load.wait()

    def widen(i, carry):
        s, q = i // blocks, lax.rem(i, blocks)
        lanes = pl.ds(pl.multiple_of(q * LANES, LANES), LANES)
        ext[s, q, pl.ds(PAD, rows), :] = proj[s, :, lanes].astype(jnp.float32)
        return carry

    lax.fori_loop(0, 3 * blocks, widen, 0)

    def short(s, q, first):
        lanes = pl.ds(pl.multiple_of(q * LANES, LANES), LANES)
        taps = taps_ref[s, :, lanes]
        value = taps[0:1, :] * ext[s, q, pl.ds(first + PAD, LANES), :]
        for j in range(1, TAPS):
            value = value + taps[j : j + 1, :] * ext[s, q, pl.ds(first + PAD - j, LANES), :]
        return value

    def products(first):
        def one(q, carry):
            value = short(1, q, first) * short(2, q, first)
            out_rows = pl.ds(pl.multiple_of(q * LANES, LANES), LANES)
            product_out[out_rows, first : first + LANES] = value.T.astype(jnp.bfloat16)
            return carry

        lax.fori_loop(0, blocks, one, 0)

        def send(k, carry):
            to = peer(k)
            pltpu.make_async_remote_copy(
                src_ref=product_out.at[pl.ds(to * share, share), pl.ds(first, LANES)],
                dst_ref=product_in.at[pl.ds(me * share, share), pl.ds(first, LANES)],
                send_sem=product_sem.at[0],
                recv_sem=product_sem.at[1],
                device_id={"seq": to},
                device_id_type=MESH,
            ).start()
            return carry

        lax.fori_loop(1, count, send, 0)
        mine = pl.ds(me * share, share)
        pltpu.make_async_copy(
            product_out.at[mine, pl.ds(first, LANES)],
            product_in.at[mine, pl.ds(first, LANES)],
            product_sem.at[1],
        ).start()

    products(LANES)
    halo_copy.wait()

    def extend(i, carry):
        s, q = i // blocks, lax.rem(i, blocks)
        lanes = pl.ds(pl.multiple_of(q * LANES, LANES), LANES)
        before = halo[s, :, lanes].astype(jnp.float32)
        ext[s, q, 0:PAD, :] = jnp.where(me == 0, 0.0, before)
        return carry

    lax.fori_loop(0, 3 * blocks, extend, 0)
    products(0)

    def queries(q, carry):
        for first in (0, LANES):
            query[q, first : first + LANES, :] = short(0, q, first)
        return carry

    lax.fori_loop(0, blocks, queries, 0)

    pltpu.make_async_copy(filt_all.at[pl.ds(1, count)], filt_all.at[pl.ds(1, count)], filt_sem.at[1]).wait()
    corner = jnp.zeros((LANES, LANES), jnp.bfloat16)
    high[0, LANES:, 0:LANES] = corner
    low[0, LANES:, 0:LANES] = corner

    def spread(d, carry):
        before, here = filt_all[d], filt_all[d + 1]
        line = jnp.concatenate([before[:, rows - LANES :], here], axis=1)
        line = jnp.where(group_of == 0, line[0:1], line[1:2])
        wide = jnp.broadcast_to(line, (LANES, line.shape[1]))
        value = pltpu.roll(wide, 0, 1, stride=1, stride_axis=0)[:, LANES:]
        top = value.astype(jnp.bfloat16)
        rest = (value - top.astype(jnp.float32)).astype(jnp.bfloat16)
        for table, part in ((high, top), (low, rest)):
            table[d, 0:LANES, :] = part
            table[d, LANES:, LANES:] = part[:, :LANES]
            table[d + 1, LANES:, :LANES] = part[:, LANES:]
        return carry

    lax.fori_loop(0, count, spread, 0)

    pltpu.make_async_copy(product_in, product_in, product_sem.at[1]).wait()
    for d in range(count):
        left = product_in[0 : channels - share * d, :]
        part = jnp.dot(left, high[d], preferred_element_type=jnp.float32)
        part = part + jnp.dot(left, low[d], preferred_element_type=jnp.float32)
        if d == 0:
            total[...] = part
        else:
            total[share * d :, :] += part
    conv_out[...] = total[...].astype(jnp.bfloat16)

    def send_back(k, carry):
        to = peer(k)
        pltpu.make_async_remote_copy(
            src_ref=conv_out.at[pl.ds(to * share, share), :],
            dst_ref=conv_in.at[pl.ds(me * share, share), :],
            send_sem=conv_send.at[0],
            recv_sem=conv_recv.at[me // per_block],
            device_id={"seq": to},
            device_id_type=MESH,
        ).start()
        return carry

    mine = pl.ds(me * share, share)
    pltpu.make_async_copy(conv_out.at[mine], conv_in.at[mine], conv_recv.at[me // per_block]).start()
    lax.fori_loop(1, count, send_back, 0)

    def pass_on(source, block, to):
        pltpu.make_async_remote_copy(
            src_ref=gated.at[source, block],
            dst_ref=gated.at[source, block],
            send_sem=gated_send.at[0],
            recv_sem=gated_recv.at[source, block],
            device_id={"chan": to},
            device_id_type=MESH,
        ).start()

    def arrived(source, block):
        slot = gated.at[source, block]
        pltpu.make_async_copy(slot, slot, gated_recv.at[source, block]).wait()

    def block_at(k):
        return lax.rem(x + blocks - k, blocks)

    def gate(k):
        block = block_at(k)
        part = pl.ds(pl.multiple_of(block * LANES, LANES), LANES)
        pltpu.make_async_copy(conv_in.at[part], conv_in.at[part], conv_recv.at[block]).wait()
        value = conv_in[part, :].astype(jnp.float32).T
        gated[chan, block] = (value * query[block]).astype(jnp.bfloat16)
        for to in (down, up, sibling):
            pass_on(chan, block, to)

    def relay_near(k):
        block = block_at(k)
        arrived(up, block)
        pass_on(up, block, down)
        pass_on(up, block, sibling)
        arrived(down, block)
        pass_on(down, block, sibling)

    def relay_far(k):
        block = block_at(k)
        arrived(far, block)
        pass_on(far, block, sibling)

    def project(k):
        block = block_at(k)
        for offset in range(heights):
            arrived(lax.rem(y + offset, heights) * 2 + 1 - core, block)
        left = jnp.concatenate([gated[c, block] for c in range(2 * heights)], axis=1)
        right = jnp.concatenate(
            [
                weight[pl.ds(pl.multiple_of(c * channels + block * LANES, LANES), LANES), :]
                for c in range(2 * heights)
            ],
            axis=0,
        )
        part = jnp.dot(left, right, preferred_element_type=jnp.float32)
        if k == 0:
            out_total[...] = part
        elif k < blocks - 1:
            out_total[...] += part
        else:
            out_ref[...] = (out_total[...] + part).astype(jnp.bfloat16)

    for k in range(blocks + 3):
        if k < blocks:
            gate(k)
        if 1 <= k <= blocks:
            relay_near(k - 1)
        if 2 <= k <= blocks + 1:
            relay_far(k - 2)
        if k == 3:
            load_weight.wait()
        if k >= 3:
            project(k - 3)

    halo_rest = product_out.at[pl.ds(0, (count - 1) * share), :]
    pltpu.make_async_copy(halo_rest, halo_rest, product_sem.at[0]).wait()
    pltpu.make_async_copy(halo_rest, halo_rest, conv_send.at[0]).wait()
    filters_sent = filt_all.at[pl.ds(1, count - 1)]
    pltpu.make_async_copy(filters_sent, filters_sent, filt_sem.at[0]).wait()
    gated_sent = gated.at[pl.ds(0, 7)]
    pltpu.make_async_copy(gated_sent, gated_sent, gated_send.at[0]).wait()


def solution(mesh):
    count = mesh.shape["seq"]
    chans = mesh.shape["chan"]
    planes, rings = 4, count // 4

    def per_device(projections, short_taps, filters, out_weight):
        rows, channels = projections.shape[1], projections.shape[2]
        blocks = channels // LANES
        vmem = pl.BlockSpec(memory_space=pltpu.VMEM)
        hbm = pl.BlockSpec(memory_space=pl.ANY)
        bf16, f32 = jnp.bfloat16, jnp.float32
        dma = pltpu.SemaphoreType.DMA
        return pl.pallas_call(
            functools.partial(kernel, (count, planes, rings)),
            out_shape=jax.ShapeDtypeStruct((rows, out_weight.shape[1]), bf16),
            in_specs=[hbm, vmem, vmem, hbm],
            out_specs=vmem,
            scratch_shapes=[
                pltpu.VMEM(projections.shape, bf16),
                pltpu.VMEM((3, PAD, channels), bf16),
                pltpu.VMEM((3, blocks, PAD + rows, LANES), f32),
                pltpu.VMEM((count + 1, filters.shape[0], rows), f32),
                pltpu.VMEM((count + 1, rows, rows), bf16),
                pltpu.VMEM((count + 1, rows, rows), bf16),
                pltpu.VMEM((channels, rows), bf16),
                pltpu.VMEM((channels, rows), bf16),
                pltpu.VMEM((channels, rows), f32),
                pltpu.VMEM((channels, rows), bf16),
                pltpu.VMEM((channels, rows), bf16),
                pltpu.VMEM((blocks, rows, LANES), f32),
                pltpu.VMEM((chans, blocks, rows, LANES), bf16),
                pltpu.VMEM(out_weight.shape, bf16),
                pltpu.VMEM((rows, out_weight.shape[1]), f32),
                dma((2,)),
                dma((1,)),
                dma((2,)),
                dma((2,)),
                dma((2,)),
                dma((1,)),
                dma((blocks,)),
                dma((1,)),
                dma((chans, blocks)),
            ],
            compiler_params=pltpu.CompilerParams(
                collective_id=0, has_side_effects=True, vmem_limit_bytes=56 * 2**20
            ),
        )(projections, short_taps, filters, out_weight)

    return jax.shard_map(
        per_device,
        mesh=mesh,
        in_specs=(P(None, "seq", "chan"), P(None, None, "chan"), P("chan", "seq"), P(None, "chan")),
        out_specs=P("seq", "chan"),
        check_vma=False,
    )
```

```python
import functools

import jax
import jax.numpy as jnp
from jax import lax
from jax.experimental import pallas as pl
from jax.experimental.pallas import tpu as pltpu
from jax.sharding import PartitionSpec as P

MESH = pl.DeviceIdType.MESH
TAPS = 7
PAD = 16
LANES = 128


def kernel(
    sizes,
    proj_hbm,
    taps_ref,
    filt_ref,
    weight_hbm,
    out_ref,
    proj,
    halo,
    ext,
    filt_mine,
    filt_all,
    high,
    low,
    early,
    product_out,
    product_in,
    total,
    conv_out,
    conv_in,
    query,
    gated,
    weight,
    out_total,
    load_sem,
    halo_sem,
    filt_sem,
    product_send,
    product_recv,
    conv_send,
    conv_recv,
    gated_send,
    gated_recv,
):
    count, planes, rings = sizes
    rows = proj.shape[1]
    channels = proj.shape[2]
    share = channels // count
    blocks = channels // LANES
    per_block = count // blocks
    groups = filt_ref.shape[0]
    me = lax.axis_index("seq")
    chan = lax.axis_index("chan")
    x, z = me // rings, lax.rem(me, rings)
    y, core = chan // 2, lax.rem(chan, 2)
    heights = lax.axis_size("chan") // 2
    step_up = 1 - 2 * core
    down = lax.rem(y + step_up + heights, heights) * 2 + core
    up = lax.rem(y - step_up + heights, heights) * 2 + core
    far = lax.rem(y + 2, heights) * 2 + core
    sibling = y * 2 + 1 - core
    following = lax.rem(me + 1, count)
    mine = pl.ds(me * share, share)

    def ring_peer(dx, k):
        side = 1 - 2 * lax.rem(k, 2)
        dz = rings // 2 + side * ((k + 1) // 2)
        return lax.rem(x + dx, planes) * rings + lax.rem(z + dz, rings)

    def far_first(k):
        return ring_peer(lax.rem(k // rings + 2, planes), lax.rem(k, rings))

    def near_first(k):
        return ring_peer(k // rings, lax.rem(k, rings))

    def each_peer(order, skip, step):
        def one(k, carry):
            step(order(k))
            return carry

        lax.fori_loop(0, skip, one, 0)
        lax.fori_loop(skip + 1, count, one, 0)

    last_of = {far_first: 2 * rings + rings - 1, near_first: rings - 1}

    def to_all(order, step):
        each_peer(order, last_of[order], step)

    barrier = pltpu.get_barrier_semaphore()

    def greet(to):
        pl.semaphore_signal(barrier, inc=1, device_id={"seq": to}, device_id_type=MESH)

    to_all(far_first, greet)
    for other in (down, up, sibling):
        pl.semaphore_signal(barrier, inc=1, device_id={"chan": other}, device_id_type=MESH)

    load_pair = pltpu.make_async_copy(proj_hbm.at[1:3], proj.at[1:3], load_sem.at[0])
    load_pair.start()
    load_query = pltpu.make_async_copy(proj_hbm.at[0], proj.at[0], load_sem.at[1])
    load_query.start()
    load_weight = pltpu.make_async_copy(weight_hbm, weight, load_sem.at[2])

    for g in range(groups):
        filt_mine[g] = filt_ref[g : g + 1, :]
    filt_all[0] = jnp.zeros(filt_all.shape[1:], jnp.float32)
    for h in range(2):
        product_in[h, 0:share, :] = jnp.zeros((share, LANES), jnp.bfloat16)

    def widen(s):
        for q in range(blocks):
            ext[s, q, pl.ds(PAD, rows), :] = proj[s, :, q * LANES : (q + 1) * LANES].astype(jnp.float32)

    def short(s, q, first, size):
        lanes = pl.ds(pl.multiple_of(q * LANES, LANES), LANES)
        taps = taps_ref[s, :, lanes]
        value = taps[0:1, :] * ext[s, q, pl.ds(first + PAD, size), :]
        for j in range(1, TAPS):
            value = value + taps[j : j + 1, :] * ext[s, q, pl.ds(first + PAD - j, size), :]
        return value

    def each_block(step):
        def one(q, carry):
            step(q)
            return carry

        lax.fori_loop(0, blocks, one, 0)

    def block_rows(q):
        return pl.ds(pl.multiple_of(q * LANES, LANES), LANES)

    def late_products(q):
        value = short(1, q, LANES, LANES) * short(2, q, LANES, LANES)
        product_out[1, block_rows(q), :] = value.T.astype(jnp.bfloat16)

    def early_products(q):
        early[q, 8:, :] = short(1, q, 8, LANES - 8) * short(2, q, 8, LANES - 8)

    def send_products(h):
        def send(to):
            pltpu.make_async_remote_copy(
                src_ref=product_out.at[h, pl.ds(to * share, share), :],
                dst_ref=product_in.at[h, pl.ds((me + 1) * share, share), :],
                send_sem=product_send.at[0],
                recv_sem=product_recv.at[h],
                device_id={"seq": to},
                device_id_type=MESH,
            ).start()

        to_all(far_first, send)
        pltpu.make_async_copy(
            product_out.at[h, mine, :],
            product_in.at[h, pl.ds((me + 1) * share, share), :],
            product_recv.at[h],
        ).start()

    load_pair.wait()
    widen(1)
    widen(2)
    each_block(late_products)

    pl.semaphore_wait(barrier, count + 2)

    halo_copy = pltpu.make_async_remote_copy(
        src_ref=proj_hbm.at[:, pl.ds(rows - PAD, PAD), :],
        dst_ref=halo,
        send_sem=halo_sem.at[0],
        recv_sem=halo_sem.at[1],
        device_id={"seq": following},
        device_id_type=MESH,
    )
    halo_copy.start()

    def send_filter(to):
        pltpu.make_async_remote_copy(
            src_ref=filt_mine.at[to // (count // groups)],
            dst_ref=filt_all.at[me + 1],
            send_sem=filt_sem.at[0],
            recv_sem=filt_sem.at[1],
            device_id={"seq": to},
            device_id_type=MESH,
        ).start()

    to_all(far_first, send_filter)
    pltpu.make_async_copy(
        filt_mine.at[me // (count // groups)], filt_all.at[me + 1], filt_sem.at[1]
    ).start()
    send_products(1)

    each_block(early_products)
    halo_copy.wait()
    for s in (1, 2, 0):
        for q in range(blocks):
            before = halo[s, :, q * LANES : (q + 1) * LANES].astype(jnp.float32)
            ext[s, q, 0:PAD, :] = jnp.where(me == 0, 0.0, before)

    def first_products(q):
        early[q, 0:8, :] = short(1, q, 0, 8) * short(2, q, 0, 8)
        product_out[0, block_rows(q), :] = early[q].T.astype(jnp.bfloat16)

    each_block(first_products)
    send_products(0)
    load_weight.start()

    load_query.wait()
    widen(0)

    def queries(q):
        for first in (0, LANES):
            query[q, first : first + LANES, :] = short(0, q, first, LANES)

    each_block(queries)

    def spread(d):
        line = jnp.concatenate([filt_all[d][:, rows - LANES :], filt_all[d + 1]], axis=1)
        wide = jnp.broadcast_to(line, (LANES, line.shape[1]))
        value = pltpu.roll(wide, 0, 1, stride=1, stride_axis=0)[:, LANES:]
        top = value.astype(jnp.bfloat16)
        high[d] = top
        low[d] = (value - top.astype(jnp.float32)).astype(jnp.bfloat16)

    def lagged(table, d, h):
        if h == 0:
            return table[d]
        before = table[d - 1][:, LANES:] if d else jnp.zeros((LANES, LANES), jnp.bfloat16)
        return jnp.concatenate([before, table[d][:, :LANES]], axis=1)

    def convolve(d, h):
        size = channels - share * d
        left = jnp.concatenate(
            [product_in[h, share : share + size, :], product_in[h, 0:size, :]], axis=1
        )
        part = None
        for table in (high, low):
            right = jnp.concatenate([lagged(table, d, h), lagged(table, d + 1, h)], axis=0)
            more = jnp.dot(left, right, preferred_element_type=jnp.float32)
            part = more if part is None else part + more
        if d == 0 and h == 1:
            total[...] = part
        else:
            total[share * d :, :] += part

    pltpu.make_async_copy(
        filt_all.at[pl.ds(1, count)], filt_all.at[pl.ds(1, count)], filt_sem.at[1]
    ).wait()
    whole = product_in.at[1, pl.ds(share, channels), :]
    pltpu.make_async_copy(whole, whole, product_recv.at[1]).wait()
    for d in range(0, count, 2):
        spread(d)
        spread(d + 1)
        convolve(d, 1)
    whole = product_in.at[0, pl.ds(share, channels), :]
    pltpu.make_async_copy(whole, whole, product_recv.at[0]).wait()
    for d in range(0, count, 2):
        convolve(d, 0)
    conv_out[...] = total[...].astype(jnp.bfloat16)

    def send_back(to):
        pltpu.make_async_remote_copy(
            src_ref=conv_out.at[pl.ds(to * share, share), :],
            dst_ref=conv_in.at[mine, :],
            send_sem=conv_send.at[0],
            recv_sem=conv_recv.at[me // per_block],
            device_id={"seq": to},
            device_id_type=MESH,
        ).start()

    to_all(near_first, send_back)
    pltpu.make_async_copy(conv_out.at[mine], conv_in.at[mine], conv_recv.at[me // per_block]).start()

    def pass_on(source, block, to):
        pltpu.make_async_remote_copy(
            src_ref=gated.at[source, block],
            dst_ref=gated.at[source, block],
            send_sem=gated_send.at[0],
            recv_sem=gated_recv.at[source, block],
            device_id={"chan": to},
            device_id_type=MESH,
        ).start()

    def arrived(source, block):
        slot = gated.at[source, block]
        pltpu.make_async_copy(slot, slot, gated_recv.at[source, block]).wait()

    def block_at(k):
        return lax.rem(x + blocks - k, blocks)

    def gate(k):
        block = block_at(k)
        part = block_rows(block)
        pltpu.make_async_copy(conv_in.at[part], conv_in.at[part], conv_recv.at[block]).wait()
        value = conv_in[part, :].astype(jnp.float32).T
        gated[chan, block] = (value * query[block]).astype(jnp.bfloat16)
        for to in (down, up, sibling):
            pass_on(chan, block, to)

    def relay_near(k):
        block = block_at(k)
        arrived(up, block)
        pass_on(up, block, down)
        pass_on(up, block, sibling)
        arrived(down, block)
        pass_on(down, block, sibling)

    def relay_far(k):
        block = block_at(k)
        arrived(far, block)
        pass_on(far, block, sibling)

    def project(k):
        block = block_at(k)
        for offset in range(heights):
            arrived(lax.rem(y + offset, heights) * 2 + 1 - core, block)
        left = jnp.concatenate([gated[c, block] for c in range(2 * heights)], axis=1)
        right = jnp.concatenate(
            [
                weight[pl.ds(pl.multiple_of(c * channels + block * LANES, LANES), LANES), :]
                for c in range(2 * heights)
            ],
            axis=0,
        )
        part = jnp.dot(left, right, preferred_element_type=jnp.float32)
        if k == 0:
            out_total[...] = part
        elif k < blocks - 1:
            out_total[...] += part
        else:
            out_ref[...] = (out_total[...] + part).astype(jnp.bfloat16)

    load_weight.wait()
    steps = (
        (gate, 0), (gate, 1), (gate, 2), (relay_near, 0), (gate, 3), (relay_near, 1),
        (relay_near, 2), (relay_far, 0), (relay_near, 3), (relay_far, 1), (project, 0),
        (relay_far, 2), (project, 1), (relay_far, 3), (project, 2), (project, 3),
    )
    for step, k in steps:
        step(k)

    sent = product_out.at[0:2, pl.ds(0, (count - 1) * share), :]
    pltpu.make_async_copy(sent, sent, product_send.at[0]).wait()
    sent = conv_out.at[pl.ds(0, (count - 1) * share), :]
    pltpu.make_async_copy(sent, sent, conv_send.at[0]).wait()
    sent = filt_all.at[pl.ds(1, count - 1)]
    pltpu.make_async_copy(sent, sent, filt_sem.at[0]).wait()
    sent = gated.at[pl.ds(0, 7)]
    pltpu.make_async_copy(sent, sent, gated_send.at[0]).wait()


def solution(mesh):
    count = mesh.shape["seq"]
    chans = mesh.shape["chan"]
    planes, rings = 4, count // 4

    def per_device(projections, short_taps, filters, out_weight):
        rows, channels = projections.shape[1], projections.shape[2]
        blocks = channels // LANES
        share = channels // count
        vmem = pl.BlockSpec(memory_space=pltpu.VMEM)
        hbm = pl.BlockSpec(memory_space=pl.ANY)
        bf16, f32 = jnp.bfloat16, jnp.float32
        dma = pltpu.SemaphoreType.DMA
        return pl.pallas_call(
            functools.partial(kernel, (count, planes, rings)),
            out_shape=jax.ShapeDtypeStruct((rows, out_weight.shape[1]), bf16),
            in_specs=[hbm, vmem, vmem, hbm],
            out_specs=vmem,
            scratch_shapes=[
                pltpu.VMEM(projections.shape, bf16),
                pltpu.VMEM((3, PAD, channels), bf16),
                pltpu.VMEM((3, blocks, PAD + rows, LANES), f32),
                pltpu.VMEM((filters.shape[0], 1, rows), f32),
                pltpu.VMEM((count + 1, 1, rows), f32),
                pltpu.VMEM((count, LANES, rows), bf16),
                pltpu.VMEM((count, LANES, rows), bf16),
                pltpu.VMEM((blocks, LANES, LANES), f32),
                pltpu.VMEM((2, channels, LANES), bf16),
                pltpu.VMEM((2, share + channels, LANES), bf16),
                pltpu.VMEM((channels, rows), f32),
                pltpu.VMEM((channels, rows), bf16),
                pltpu.VMEM((channels, rows), bf16),
                pltpu.VMEM((blocks, rows, LANES), f32),
                pltpu.VMEM((chans, blocks, rows, LANES), bf16),
                pltpu.VMEM(out_weight.shape, bf16),
                pltpu.VMEM((rows, out_weight.shape[1]), f32),
                dma((3,)),
                dma((2,)),
                dma((2,)),
                dma((1,)),
                dma((2,)),
                dma((1,)),
                dma((blocks,)),
                dma((1,)),
                dma((chans, blocks)),
            ],
            compiler_params=pltpu.CompilerParams(
                collective_id=0, has_side_effects=True, vmem_limit_bytes=56 * 2**20
            ),
        )(projections, short_taps, filters, out_weight)

    return jax.shard_map(
        per_device,
        mesh=mesh,
        in_specs=(P(None, "seq", "chan"), P(None, None, "chan"), P("chan", "seq"), P(None, "chan")),
        out_specs=P("seq", "chan"),
        check_vma=False,
    )
```

```python
import functools

import jax
import jax.numpy as jnp
from jax import lax
from jax.experimental import pallas as pl
from jax.experimental.pallas import tpu as pltpu
from jax.sharding import PartitionSpec as P

MESH = pl.DeviceIdType.MESH
TAPS = 7
PAD = 16
LANES = 128


def kernel(
    sizes,
    proj_hbm,
    taps_hbm,
    filt_hbm,
    weight_hbm,
    out_ref,
    taps_ref,
    filt_ref,
    proj,
    halo,
    ext,
    filt_mine,
    filt_all,
    high,
    low,
    early,
    product_out,
    product_in,
    total,
    conv_out,
    conv_in,
    query,
    gated,
    weight,
    out_total,
    load_sem,
    halo_sem,
    filt_sem,
    product_send,
    product_recv,
    conv_send,
    conv_recv,
    gated_send,
    gated_recv,
):
    count, planes, rings = sizes
    rows = proj.shape[1]
    channels = proj.shape[2]
    share = channels // count
    blocks = channels // LANES
    per_block = count // blocks
    groups = filt_ref.shape[0]
    me = lax.axis_index("seq")
    chan = lax.axis_index("chan")
    x, z = me // rings, lax.rem(me, rings)
    y, core = chan // 2, lax.rem(chan, 2)
    heights = lax.axis_size("chan") // 2
    step_up = 1 - 2 * core
    down = lax.rem(y + step_up + heights, heights) * 2 + core
    up = lax.rem(y - step_up + heights, heights) * 2 + core
    far = lax.rem(y + 2, heights) * 2 + core
    sibling = y * 2 + 1 - core
    following = lax.rem(me + 1, count)
    mine = pl.ds(me * share, share)

    def ring_peer(dx, k):
        side = 1 - 2 * lax.rem(k, 2)
        dz = rings // 2 + side * ((k + 1) // 2)
        return lax.rem(x + dx, planes) * rings + lax.rem(z + dz, rings)

    def far_first(k):
        return ring_peer(lax.rem(k // rings + 2, planes), lax.rem(k, rings))

    def near_first(k):
        return ring_peer(k // rings, lax.rem(k, rings))

    def each_peer(order, skip, step):
        def one(k, carry):
            step(order(k))
            return carry

        lax.fori_loop(0, skip, one, 0)
        lax.fori_loop(skip + 1, count, one, 0)

    last_of = {far_first: 2 * rings + rings - 1, near_first: rings - 1}

    def to_all(order, step):
        each_peer(order, last_of[order], step)

    barrier = pltpu.get_barrier_semaphore()

    def greet(to):
        pl.semaphore_signal(barrier, inc=1, device_id={"seq": to}, device_id_type=MESH)

    to_all(far_first, greet)
    for other in (down, up, sibling):
        pl.semaphore_signal(barrier, inc=1, device_id={"chan": other}, device_id_type=MESH)

    load_taps = pltpu.make_async_copy(taps_hbm, taps_ref, load_sem.at[3])
    load_taps.start()
    load_filt = pltpu.make_async_copy(filt_hbm, filt_ref, load_sem.at[4])
    load_filt.start()
    load_pair = pltpu.make_async_copy(proj_hbm.at[1:3], proj.at[1:3], load_sem.at[0])
    load_pair.start()
    load_query = pltpu.make_async_copy(proj_hbm.at[0], proj.at[0], load_sem.at[1])
    load_query.start()
    load_weight = pltpu.make_async_copy(weight_hbm, weight, load_sem.at[2])

    for h in range(2):
        product_in[h, 0:LANES, :] = jnp.zeros((LANES, LANES), jnp.bfloat16)

    def widen(s):
        for q in range(blocks):
            ext[s, q, pl.ds(PAD, rows), :] = proj[s, :, q * LANES : (q + 1) * LANES].astype(jnp.float32)

    def short(s, q, first, size):
        lanes = pl.ds(pl.multiple_of(q * LANES, LANES), LANES)
        taps = taps_ref[s, :, lanes]
        value = taps[0:1, :] * ext[s, q, pl.ds(first + PAD, size), :]
        for j in range(1, TAPS):
            value = value + taps[j : j + 1, :] * ext[s, q, pl.ds(first + PAD - j, size), :]
        return value

    def each_block(step):
        def one(q, carry):
            step(q)
            return carry

        lax.fori_loop(0, blocks, one, 0)

    def block_rows(q):
        return pl.ds(pl.multiple_of(q * LANES, LANES), LANES)

    def late_products(q):
        value = short(1, q, LANES, LANES) * short(2, q, LANES, LANES)
        product_out[1, block_rows(q), :] = value.T.astype(jnp.bfloat16)

    def early_products(q):
        early[q, 8:, :] = short(1, q, 8, LANES - 8) * short(2, q, 8, LANES - 8)

    def send_products(h):
        def send(to):
            pltpu.make_async_remote_copy(
                src_ref=product_out.at[h, pl.ds(to * share, share), :],
                dst_ref=product_in.at[h, pl.ds(LANES + me * share, share), :],
                send_sem=product_send.at[0],
                recv_sem=product_recv.at[h],
                device_id={"seq": to},
                device_id_type=MESH,
            ).start()

        to_all(far_first, send)
        pltpu.make_async_copy(
            product_out.at[h, mine, :],
            product_in.at[h, pl.ds(LANES + me * share, share), :],
            product_recv.at[h],
        ).start()

    load_taps.wait()
    load_pair.wait()
    widen(1)
    widen(2)
    each_block(late_products)

    load_filt.wait()
    for g in range(groups):
        filt_mine[g] = filt_ref[g : g + 1, :]
    filt_all[0] = jnp.zeros(filt_all.shape[1:], jnp.float32)
    pl.semaphore_wait(barrier, count + 2)

    def halo_of(part, at):
        return pltpu.make_async_remote_copy(
            src_ref=proj.at[part, pl.ds(rows - PAD, PAD), :],
            dst_ref=halo.at[part],
            send_sem=halo_sem.at[at],
            recv_sem=halo_sem.at[at + 1],
            device_id={"seq": following},
            device_id_type=MESH,
        )

    pair_halo = halo_of(pl.ds(1, 2), 0)
    pair_halo.start()

    def send_filter(to):
        pltpu.make_async_remote_copy(
            src_ref=filt_mine.at[to // (count // groups)],
            dst_ref=filt_all.at[me + 1],
            send_sem=filt_sem.at[0],
            recv_sem=filt_sem.at[1],
            device_id={"seq": to},
            device_id_type=MESH,
        ).start()

    to_all(far_first, send_filter)
    pltpu.make_async_copy(
        filt_mine.at[me // (count // groups)], filt_all.at[me + 1], filt_sem.at[1]
    ).start()
    send_products(1)

    each_block(early_products)
    def extend(s):
        for q in range(blocks):
            before = halo[s, :, q * LANES : (q + 1) * LANES].astype(jnp.float32)
            ext[s, q, 0:PAD, :] = jnp.where(me == 0, 0.0, before)

    pair_halo.wait()
    extend(1)
    extend(2)

    def first_products(q):
        early[q, 0:8, :] = short(1, q, 0, 8) * short(2, q, 0, 8)
        product_out[0, block_rows(q), :] = early[q].T.astype(jnp.bfloat16)

    each_block(first_products)
    send_products(0)
    load_weight.start()

    query_halo = halo_of(0, 2)
    load_query.wait()
    query_halo.start()
    widen(0)
    query_halo.wait()
    extend(0)

    def queries(q):
        for first in (0, LANES):
            query[q, first : first + LANES, :] = short(0, q, first, LANES)

    each_block(queries)

    def spread(d):
        line = jnp.concatenate([filt_all[d][:, rows - LANES :], filt_all[d + 1]], axis=1)
        wide = jnp.broadcast_to(line, (LANES, line.shape[1]))
        value = pltpu.roll(wide, 0, 1, stride=1, stride_axis=0)[:, LANES:]
        top = value.astype(jnp.bfloat16)
        high[d] = top
        low[d] = (value - top.astype(jnp.float32)).astype(jnp.bfloat16)

    def lagged(table, d):
        before = table[d - 1][:, LANES:] if d else jnp.zeros((LANES, LANES), jnp.bfloat16)
        return jnp.concatenate([before, table[d][:, :LANES]], axis=1)

    def convolve_late(d):
        size = channels - share * d
        left = jnp.concatenate(
            [
                product_in[1, LANES : LANES + size, :],
                product_in[1, LANES - share : LANES - share + size, :],
            ],
            axis=1,
        )
        part = None
        for table in (high, low):
            right = jnp.concatenate([lagged(table, d), lagged(table, d + 1)], axis=0)
            more = jnp.dot(left, right, preferred_element_type=jnp.float32)
            part = more if part is None else part + more
        if d == 0:
            total[...] = part
        else:
            total[share * d :, :] += part

    def convolve_early(block):
        base = pl.multiple_of(block * LANES, LANES)

        def lags(step, value):
            for e in range(0, per_block, 2):
                d = step * per_block + e
                first = LANES + base - share * d
                left = jnp.concatenate(
                    [
                        product_in[0, pl.ds(pl.multiple_of(first, share), LANES), :],
                        product_in[0, pl.ds(pl.multiple_of(first - share, share), LANES), :],
                    ],
                    axis=1,
                )
                for table in (high, low):
                    right = table[pl.ds(d, 2)].reshape(2 * LANES, rows)
                    value = value + jnp.dot(left, right, preferred_element_type=jnp.float32)
            return value

        value = lax.fori_loop(0, block + 1, lags, total[pl.ds(base, LANES), :])
        conv_out[pl.ds(base, LANES), :] = value.astype(jnp.bfloat16)

    pltpu.make_async_copy(
        filt_all.at[pl.ds(1, count)], filt_all.at[pl.ds(1, count)], filt_sem.at[1]
    ).wait()
    whole = product_in.at[1, pl.ds(LANES, channels), :]
    pltpu.make_async_copy(whole, whole, product_recv.at[1]).wait()
    for d in range(0, count, 2):
        spread(d)
        spread(d + 1)
        convolve_late(d)
    whole = product_in.at[0, pl.ds(LANES, channels), :]
    pltpu.make_async_copy(whole, whole, product_recv.at[0]).wait()
    def send_back(to):
        pltpu.make_async_remote_copy(
            src_ref=conv_out.at[pl.ds(to * share, share), :],
            dst_ref=conv_in.at[mine, :],
            send_sem=conv_send.at[0],
            recv_sem=conv_recv.at[me // per_block],
            device_id={"seq": to},
            device_id_type=MESH,
        ).start()

    for k in range(blocks):
        convolve_early(lax.rem(x + k, blocks))

        def one(i, carry):
            send_back(near_first(k * rings + i))
            return carry

        lax.fori_loop(0, rings - 1 if k == 0 else rings, one, 0)
        if k == 0:
            own = conv_recv.at[me // per_block]
            pltpu.make_async_copy(conv_out.at[mine], conv_in.at[mine], own).start()

    def pass_on(source, block, to):
        pltpu.make_async_remote_copy(
            src_ref=gated.at[source, block],
            dst_ref=gated.at[source, block],
            send_sem=gated_send.at[0],
            recv_sem=gated_recv.at[source, block],
            device_id={"chan": to},
            device_id_type=MESH,
        ).start()

    def arrived(source, block):
        slot = gated.at[source, block]
        pltpu.make_async_copy(slot, slot, gated_recv.at[source, block]).wait()

    def block_at(k):
        return lax.rem(x + blocks - k, blocks)

    def gate(k):
        block = block_at(k)
        part = block_rows(block)
        pltpu.make_async_copy(conv_in.at[part], conv_in.at[part], conv_recv.at[block]).wait()
        value = conv_in[part, :].astype(jnp.float32).T
        gated[chan, block] = (value * query[block]).astype(jnp.bfloat16)
        for to in (down, sibling):
            pass_on(chan, block, to)

    def send_up(k):
        pass_on(chan, block_at(k), up)

    def near_up(k):
        block = block_at(k)
        arrived(up, block)
        pass_on(up, block, down)
        pass_on(up, block, sibling)

    def near_down(k):
        block = block_at(k)
        arrived(down, block)
        pass_on(down, block, sibling)

    def relay_far(k):
        block = block_at(k)
        arrived(far, block)
        pass_on(far, block, sibling)

    def project_part(k, stream):
        block = block_at(k)
        sources = [
            lax.rem(y + offset, heights) * 2 + (1 - core if stream else core)
            for offset in range(heights)
        ]
        left = jnp.concatenate([gated[c, block] for c in sources], axis=1)
        right = jnp.concatenate(
            [
                weight[pl.ds(pl.multiple_of(c * channels + block * LANES, LANES), LANES), :]
                for c in sources
            ],
            axis=0,
        )
        return jnp.dot(left, right, preferred_element_type=jnp.float32)

    def project_mine(k):
        part = project_part(k, 0)
        if k == 0:
            out_total[...] = part
        else:
            out_total[...] += part

    def project_other(k):
        block = block_at(k)
        for offset in range(heights):
            arrived(lax.rem(y + offset, heights) * 2 + 1 - core, block)
        part = project_part(k, 1)
        if k < blocks - 1:
            out_total[...] += part
        else:
            out_ref[...] = (out_total[...] + part).astype(jnp.bfloat16)

    load_weight.wait()
    steps = (
        (gate, 0), (send_up, 0), (gate, 1), (send_up, 1), (gate, 2),
        (send_up, 2), (gate, 3), (send_up, 3), (near_up, 0), (near_up, 1),
        (near_up, 2), (near_up, 3), (near_down, 0), (near_down, 1), (near_down, 2),
        (near_down, 3), (relay_far, 0), (relay_far, 1), (project_mine, 0), (relay_far, 2),
        (project_other, 0), (project_mine, 1), (relay_far, 3), (project_other, 1), (project_mine, 2),
        (project_mine, 3), (project_other, 2), (project_other, 3),
    )
    for step, k in steps:
        step(k)

    sent = product_out.at[0:2, pl.ds(0, (count - 1) * share), :]
    pltpu.make_async_copy(sent, sent, product_send.at[0]).wait()
    sent = conv_out.at[pl.ds(0, (count - 1) * share), :]
    pltpu.make_async_copy(sent, sent, conv_send.at[0]).wait()
    sent = filt_all.at[pl.ds(1, count - 1)]
    pltpu.make_async_copy(sent, sent, filt_sem.at[0]).wait()
    sent = gated.at[pl.ds(0, 7)]
    pltpu.make_async_copy(sent, sent, gated_send.at[0]).wait()


def solution(mesh):
    count = mesh.shape["seq"]
    chans = mesh.shape["chan"]
    planes, rings = 4, count // 4

    def per_device(projections, short_taps, filters, out_weight):
        rows, channels = projections.shape[1], projections.shape[2]
        blocks = channels // LANES
        share = channels // count
        vmem = pl.BlockSpec(memory_space=pltpu.VMEM)
        hbm = pl.BlockSpec(memory_space=pl.ANY)
        bf16, f32 = jnp.bfloat16, jnp.float32
        dma = pltpu.SemaphoreType.DMA
        return pl.pallas_call(
            functools.partial(kernel, (count, planes, rings)),
            out_shape=jax.ShapeDtypeStruct((rows, out_weight.shape[1]), bf16),
            in_specs=[hbm, hbm, hbm, hbm],
            out_specs=vmem,
            scratch_shapes=[
                pltpu.VMEM(short_taps.shape, f32),
                pltpu.VMEM(filters.shape, f32),
                pltpu.VMEM(projections.shape, bf16),
                pltpu.VMEM((3, PAD, channels), bf16),
                pltpu.VMEM((3, blocks, PAD + rows, LANES), f32),
                pltpu.VMEM((filters.shape[0], 1, rows), f32),
                pltpu.VMEM((count + 1, 1, rows), f32),
                pltpu.VMEM((count, LANES, rows), bf16),
                pltpu.VMEM((count, LANES, rows), bf16),
                pltpu.VMEM((blocks, LANES, LANES), f32),
                pltpu.VMEM((2, channels, LANES), bf16),
                pltpu.VMEM((2, LANES + channels, LANES), bf16),
                pltpu.VMEM((channels, rows), f32),
                pltpu.VMEM((channels, rows), bf16),
                pltpu.VMEM((channels, rows), bf16),
                pltpu.VMEM((blocks, rows, LANES), f32),
                pltpu.VMEM((chans, blocks, rows, LANES), bf16),
                pltpu.VMEM(out_weight.shape, bf16),
                pltpu.VMEM((rows, out_weight.shape[1]), f32),
                dma((5,)),
                dma((4,)),
                dma((2,)),
                dma((1,)),
                dma((2,)),
                dma((1,)),
                dma((blocks,)),
                dma((1,)),
                dma((chans, blocks)),
            ],
            compiler_params=pltpu.CompilerParams(
                collective_id=0, has_side_effects=True, vmem_limit_bytes=53 * 2**20
            ),
        )(projections, short_taps, filters, out_weight)

    return jax.shard_map(
        per_device,
        mesh=mesh,
        in_specs=(P(None, "seq", "chan"), P(None, None, "chan"), P("chan", "seq"), P(None, "chan")),
        out_specs=P("seq", "chan"),
        check_vma=False,
    )
```

```python
import functools

import jax
import jax.numpy as jnp
from jax import lax
from jax.experimental import pallas as pl
from jax.experimental.pallas import tpu as pltpu
from jax.sharding import PartitionSpec as P

MESH = pl.DeviceIdType.MESH
TAPS = 7
PAD = 16
LANES = 128


def kernel(
    sizes,
    proj_hbm,
    taps_hbm,
    filt_hbm,
    weight_hbm,
    out_ref,
    taps_ref,
    filt_ref,
    proj,
    halo,
    ext,
    filt_mine,
    filt_all,
    high,
    low,
    early,
    product_out,
    product_in,
    total,
    conv_out,
    conv_in,
    query,
    gated,
    weight,
    out_total,
    load_sem,
    halo_sem,
    filt_sem,
    product_send,
    product_recv,
    conv_send,
    conv_recv,
    gated_send,
    gated_recv,
):
    count, planes, rings = sizes
    rows = proj.shape[1]
    channels = proj.shape[2]
    share = channels // count
    blocks = channels // LANES
    per_block = count // blocks
    groups = filt_ref.shape[0]
    me = lax.axis_index("seq")
    chan = lax.axis_index("chan")
    x, z = me // rings, lax.rem(me, rings)
    y, core = chan // 2, lax.rem(chan, 2)
    heights = lax.axis_size("chan") // 2
    step_up = 1 - 2 * core
    down = lax.rem(y + step_up + heights, heights) * 2 + core
    up = lax.rem(y - step_up + heights, heights) * 2 + core
    far = lax.rem(y + 2, heights) * 2 + core
    sibling = y * 2 + 1 - core
    following = lax.rem(me + 1, count)
    mine = pl.ds(me * share, share)

    def ring_peer(dx, k):
        side = 1 - 2 * lax.rem(k, 2)
        dz = rings // 2 + side * ((k + 1) // 2)
        return lax.rem(x + dx, planes) * rings + lax.rem(z + dz, rings)

    def far_first(k):
        return ring_peer(lax.rem(k // rings + 2, planes), lax.rem(k, rings))

    def near_first(k):
        return ring_peer(k // rings, lax.rem(k, rings))

    def each_peer(order, skip, step):
        def one(k, carry):
            step(order(k))
            return carry

        lax.fori_loop(0, skip, one, 0)
        lax.fori_loop(skip + 1, count, one, 0)

    last_of = {far_first: 2 * rings + rings - 1, near_first: rings - 1}

    def to_all(order, step):
        each_peer(order, last_of[order], step)

    barrier = pltpu.get_barrier_semaphore()

    def greet(to):
        pl.semaphore_signal(barrier, inc=1, device_id={"seq": to}, device_id_type=MESH)

    to_all(far_first, greet)
    for other in (down, up, sibling):
        pl.semaphore_signal(barrier, inc=1, device_id={"chan": other}, device_id_type=MESH)

    load_taps = pltpu.make_async_copy(taps_hbm, taps_ref, load_sem.at[3])
    load_taps.start()
    load_filt = pltpu.make_async_copy(filt_hbm, filt_ref, load_sem.at[4])
    load_filt.start()
    load_pair = pltpu.make_async_copy(proj_hbm.at[1:3], proj.at[1:3], load_sem.at[0])
    load_pair.start()
    load_query = pltpu.make_async_copy(proj_hbm.at[0], proj.at[0], load_sem.at[1])
    load_query.start()
    load_weight = pltpu.make_async_copy(weight_hbm, weight, load_sem.at[2])

    for h in range(2):
        product_in[h, 0:LANES, :] = jnp.zeros((LANES, LANES), jnp.bfloat16)

    def widen(s):
        for q in range(blocks):
            ext[s, q, pl.ds(PAD, rows), :] = proj[s, :, q * LANES : (q + 1) * LANES].astype(jnp.float32)

    def short(s, q, first, size):
        lanes = pl.ds(pl.multiple_of(q * LANES, LANES), LANES)
        taps = taps_ref[s, :, lanes]
        value = taps[0:1, :] * ext[s, q, pl.ds(first + PAD, size), :]
        for j in range(1, TAPS):
            value = value + taps[j : j + 1, :] * ext[s, q, pl.ds(first + PAD - j, size), :]
        return value

    def each_block(step):
        def one(q, carry):
            step(q)
            return carry

        lax.fori_loop(0, blocks, one, 0)

    def block_rows(q):
        return pl.ds(pl.multiple_of(q * LANES, LANES), LANES)

    def late_products(q):
        value = short(1, q, LANES, LANES) * short(2, q, LANES, LANES)
        product_out[1, block_rows(q), :] = value.T.astype(jnp.bfloat16)

    def early_products(q):
        early[q, 8:, :] = short(1, q, 8, LANES - 8) * short(2, q, 8, LANES - 8)

    def send_products(h):
        def send(to):
            pltpu.make_async_remote_copy(
                src_ref=product_out.at[h, pl.ds(to * share, share), :],
                dst_ref=product_in.at[h, pl.ds(LANES + me * share, share), :],
                send_sem=product_send.at[0],
                recv_sem=product_recv.at[h],
                device_id={"seq": to},
                device_id_type=MESH,
            ).start()

        to_all(far_first, send)
        pltpu.make_async_copy(
            product_out.at[h, mine, :],
            product_in.at[h, pl.ds(LANES + me * share, share), :],
            product_recv.at[h],
        ).start()

    load_taps.wait()
    load_pair.wait()
    widen(1)
    widen(2)
    each_block(late_products)

    load_filt.wait()
    for g in range(groups):
        filt_mine[g] = filt_ref[g : g + 1, :]
    filt_all[0] = jnp.zeros(filt_all.shape[1:], jnp.float32)
    pl.semaphore_wait(barrier, count + 2)

    def halo_of(part, at):
        return pltpu.make_async_remote_copy(
            src_ref=proj.at[part, pl.ds(rows - PAD, PAD), :],
            dst_ref=halo.at[part],
            send_sem=halo_sem.at[at],
            recv_sem=halo_sem.at[at + 1],
            device_id={"seq": following},
            device_id_type=MESH,
        )

    pair_halo = halo_of(pl.ds(1, 2), 0)
    pair_halo.start()

    def send_filter(to):
        pltpu.make_async_remote_copy(
            src_ref=filt_mine.at[to // (count // groups)],
            dst_ref=filt_all.at[me + 1],
            send_sem=filt_sem.at[0],
            recv_sem=filt_sem.at[1],
            device_id={"seq": to},
            device_id_type=MESH,
        ).start()

    to_all(far_first, send_filter)
    pltpu.make_async_copy(
        filt_mine.at[me // (count // groups)], filt_all.at[me + 1], filt_sem.at[1]
    ).start()
    send_products(1)

    each_block(early_products)
    def extend(s):
        for q in range(blocks):
            before = halo[s, :, q * LANES : (q + 1) * LANES].astype(jnp.float32)
            ext[s, q, 0:PAD, :] = jnp.where(me == 0, 0.0, before)

    pair_halo.wait()
    extend(1)
    extend(2)

    def first_products(q):
        early[q, 0:8, :] = short(1, q, 0, 8) * short(2, q, 0, 8)
        product_out[0, block_rows(q), :] = early[q].T.astype(jnp.bfloat16)

    each_block(first_products)
    send_products(0)
    load_weight.start()

    query_halo = halo_of(0, 2)
    load_query.wait()
    query_halo.start()
    widen(0)
    def spread(d):
        line = jnp.concatenate([filt_all[d][:, rows - LANES :], filt_all[d + 1]], axis=1)
        wide = jnp.broadcast_to(line, (LANES, line.shape[1]))
        value = pltpu.roll(wide, 0, 1, stride=1, stride_axis=0)[:, LANES:]
        top = value.astype(jnp.bfloat16)
        high[d] = top
        low[d] = (value - top.astype(jnp.float32)).astype(jnp.bfloat16)

    def lagged(table, d):
        before = table[d - 1][:, LANES:] if d else jnp.zeros((LANES, LANES), jnp.bfloat16)
        return jnp.concatenate([before, table[d][:, :LANES]], axis=1)

    def convolve_late(d):
        size = channels - share * d
        left = jnp.concatenate(
            [
                product_in[1, LANES : LANES + size, :],
                product_in[1, LANES - share : LANES - share + size, :],
            ],
            axis=1,
        )
        part = None
        for table in (high, low):
            right = jnp.concatenate([lagged(table, d), lagged(table, d + 1)], axis=0)
            more = jnp.dot(left, right, preferred_element_type=jnp.float32)
            part = more if part is None else part + more
        if d == 0:
            total[...] = part
        else:
            total[share * d :, :] += part

    def convolve_early(block):
        base = pl.multiple_of(block * LANES, LANES)

        def lags(step, value):
            for e in range(0, per_block, 2):
                d = step * per_block + e
                first = LANES + base - share * d
                left = jnp.concatenate(
                    [
                        product_in[0, pl.ds(pl.multiple_of(first, share), LANES), :],
                        product_in[0, pl.ds(pl.multiple_of(first - share, share), LANES), :],
                    ],
                    axis=1,
                )
                for table in (high,):
                    right = table[pl.ds(d, 2)].reshape(2 * LANES, rows)
                    value = value + jnp.dot(left, right, preferred_element_type=jnp.float32)
            return value

        value = lax.fori_loop(0, block + 1, lags, total[pl.ds(base, LANES), :])
        conv_out[pl.ds(base, LANES), :] = value.astype(jnp.bfloat16)

    pltpu.make_async_copy(
        filt_all.at[pl.ds(1, count)], filt_all.at[pl.ds(1, count)], filt_sem.at[1]
    ).wait()
    for d in range(count):
        spread(d)
    whole = product_in.at[1, pl.ds(LANES, channels), :]
    pltpu.make_async_copy(whole, whole, product_recv.at[1]).wait()
    for d in range(0, count, 2):
        convolve_late(d)
    query_halo.wait()
    extend(0)

    def queries(q):
        for first in (0, LANES):
            query[q, first : first + LANES, :] = short(0, q, first, LANES)

    each_block(queries)

    whole = product_in.at[0, pl.ds(LANES, channels), :]
    pltpu.make_async_copy(whole, whole, product_recv.at[0]).wait()
    def send_back(to):
        pltpu.make_async_remote_copy(
            src_ref=conv_out.at[pl.ds(to * share, share), :],
            dst_ref=conv_in.at[mine, :],
            send_sem=conv_send.at[0],
            recv_sem=conv_recv.at[me // per_block],
            device_id={"seq": to},
            device_id_type=MESH,
        ).start()

    for k in range(blocks):
        convolve_early(lax.rem(x + k, blocks))

        def one(i, carry):
            send_back(near_first(k * rings + i))
            return carry

        lax.fori_loop(0, rings - 1 if k == 0 else rings, one, 0)
        if k == 0:
            own = conv_recv.at[me // per_block]
            pltpu.make_async_copy(conv_out.at[mine], conv_in.at[mine], own).start()

    def pass_on(source, block, to):
        pltpu.make_async_remote_copy(
            src_ref=gated.at[source, block],
            dst_ref=gated.at[source, block],
            send_sem=gated_send.at[0],
            recv_sem=gated_recv.at[source, block],
            device_id={"chan": to},
            device_id_type=MESH,
        ).start()

    def arrived(source, block):
        slot = gated.at[source, block]
        pltpu.make_async_copy(slot, slot, gated_recv.at[source, block]).wait()

    def block_at(k):
        return lax.rem(x + blocks - k, blocks)

    def gate(k):
        block = block_at(k)
        part = block_rows(block)
        pltpu.make_async_copy(conv_in.at[part], conv_in.at[part], conv_recv.at[block]).wait()
        value = conv_in[part, :].astype(jnp.float32).T
        gated[chan, block] = (value * query[block]).astype(jnp.bfloat16)
        for to in (down, sibling):
            pass_on(chan, block, to)

    def send_up(k):
        pass_on(chan, block_at(k), up)

    def near_up(k):
        block = block_at(k)
        arrived(up, block)
        pass_on(up, block, down)
        pass_on(up, block, sibling)

    def near_down(k):
        block = block_at(k)
        arrived(down, block)
        pass_on(down, block, sibling)

    def relay_far(k):
        block = block_at(k)
        arrived(far, block)
        pass_on(far, block, sibling)

    def project_part(k, stream):
        block = block_at(k)
        sources = [
            lax.rem(y + offset, heights) * 2 + (1 - core if stream else core)
            for offset in range(heights)
        ]
        left = jnp.concatenate([gated[c, block] for c in sources], axis=1)
        right = jnp.concatenate(
            [
                weight[pl.ds(pl.multiple_of(c * channels + block * LANES, LANES), LANES), :]
                for c in sources
            ],
            axis=0,
        )
        return jnp.dot(left, right, preferred_element_type=jnp.float32)

    def project_mine(k):
        part = project_part(k, 0)
        if k == 0:
            out_total[...] = part
        else:
            out_total[...] += part

    def project_other(k):
        block = block_at(k)
        for offset in range(heights):
            arrived(lax.rem(y + offset, heights) * 2 + 1 - core, block)
        part = project_part(k, 1)
        if k < blocks - 1:
            out_total[...] += part
        else:
            out_ref[...] = (out_total[...] + part).astype(jnp.bfloat16)

    load_weight.wait()
    steps = ((gate, 0), (send_up, 0), (gate, 1), (send_up, 1), (gate, 2), (send_up, 2), (gate, 3), (send_up, 3), (near_up, 0), (near_up, 1), (near_up, 2), (near_up, 3), (near_down, 0), (near_down, 1), (near_down, 2), (near_down, 3), (relay_far, 0), (relay_far, 1), (project_mine, 0), (project_other, 0), (relay_far, 2), (project_mine, 1), (project_other, 1), (project_mine, 2), (relay_far, 3), (project_other, 2), (project_mine, 3), (project_other, 3))
    for step, k in steps:
        step(k)

    sent = product_out.at[0:2, pl.ds(0, (count - 1) * share), :]
    pltpu.make_async_copy(sent, sent, product_send.at[0]).wait()
    sent = conv_out.at[pl.ds(0, (count - 1) * share), :]
    pltpu.make_async_copy(sent, sent, conv_send.at[0]).wait()
    sent = filt_all.at[pl.ds(1, count - 1)]
    pltpu.make_async_copy(sent, sent, filt_sem.at[0]).wait()
    sent = gated.at[pl.ds(0, 7)]
    pltpu.make_async_copy(sent, sent, gated_send.at[0]).wait()


def solution(mesh):
    count = mesh.shape["seq"]
    chans = mesh.shape["chan"]
    planes, rings = 4, count // 4

    def per_device(projections, short_taps, filters, out_weight):
        rows, channels = projections.shape[1], projections.shape[2]
        blocks = channels // LANES
        share = channels // count
        vmem = pl.BlockSpec(memory_space=pltpu.VMEM)
        hbm = pl.BlockSpec(memory_space=pl.ANY)
        bf16, f32 = jnp.bfloat16, jnp.float32
        dma = pltpu.SemaphoreType.DMA
        return pl.pallas_call(
            functools.partial(kernel, (count, planes, rings)),
            out_shape=jax.ShapeDtypeStruct((rows, out_weight.shape[1]), bf16),
            in_specs=[hbm, hbm, hbm, hbm],
            out_specs=vmem,
            scratch_shapes=[
                pltpu.VMEM(short_taps.shape, f32),
                pltpu.VMEM(filters.shape, f32),
                pltpu.VMEM(projections.shape, bf16),
                pltpu.VMEM((3, PAD, channels), bf16),
                pltpu.VMEM((3, blocks, PAD + rows, LANES), f32),
                pltpu.VMEM((filters.shape[0], 1, rows), f32),
                pltpu.VMEM((count + 1, 1, rows), f32),
                pltpu.VMEM((count, LANES, rows), bf16),
                pltpu.VMEM((count, LANES, rows), bf16),
                pltpu.VMEM((blocks, LANES, LANES), f32),
                pltpu.VMEM((2, channels, LANES), bf16),
                pltpu.VMEM((2, LANES + channels, LANES), bf16),
                pltpu.VMEM((channels, rows), f32),
                pltpu.VMEM((channels, rows), bf16),
                pltpu.VMEM((channels, rows), bf16),
                pltpu.VMEM((blocks, rows, LANES), f32),
                pltpu.VMEM((chans, blocks, rows, LANES), bf16),
                pltpu.VMEM(out_weight.shape, bf16),
                pltpu.VMEM((rows, out_weight.shape[1]), f32),
                dma((5,)),
                dma((4,)),
                dma((2,)),
                dma((1,)),
                dma((2,)),
                dma((1,)),
                dma((blocks,)),
                dma((1,)),
                dma((chans, blocks)),
            ],
            compiler_params=pltpu.CompilerParams(
                collective_id=0, has_side_effects=True, vmem_limit_bytes=24 * 2**20
            ),
        )(*[pltpu.with_memory_space_constraint(a, pltpu.HBM) for a in (projections, short_taps, filters, out_weight)])

    return jax.shard_map(
        per_device,
        mesh=mesh,
        in_specs=(P(None, "seq", "chan"), P(None, None, "chan"), P("chan", "seq"), P(None, "chan")),
        out_specs=P("seq", "chan"),
        check_vma=False,
    )
```

```python
import functools

import jax
import jax.numpy as jnp
from jax import lax
from jax.experimental import pallas as pl
from jax.experimental.pallas import tpu as pltpu
from jax.sharding import PartitionSpec as P

MESH = pl.DeviceIdType.MESH
TAPS = 7
BACK_ORDER = (0, 2, 1, 3)
PAD = 16
LANES = 128


def kernel(
    sizes,
    proj_hbm,
    taps_hbm,
    filt_hbm,
    weight_hbm,
    out_ref,
    taps_ref,
    filt_ref,
    proj,
    halo,
    edge_out,
    edge_in,
    ext,
    filt_mine,
    filt_all,
    high,
    low,
    early,
    product_out,
    product_in,
    total,
    conv_out,
    conv_in,
    query,
    gated,
    weight,
    out_total,
    load_sem,
    halo_sem,
    filt_sem,
    product_send,
    product_recv,
    conv_send,
    conv_recv,
    gated_send,
    gated_recv,
):
    count, planes, rings = sizes
    rows = proj.shape[1]
    channels = proj.shape[2]
    share = channels // count
    blocks = channels // LANES
    per_block = count // blocks
    groups = filt_ref.shape[0]
    me = lax.axis_index("seq")
    chan = lax.axis_index("chan")
    x, z = me // rings, lax.rem(me, rings)
    y, core = chan // 2, lax.rem(chan, 2)
    heights = lax.axis_size("chan") // 2
    step_up = 1 - 2 * core
    down = lax.rem(y + step_up + heights, heights) * 2 + core
    up = lax.rem(y - step_up + heights, heights) * 2 + core
    far = lax.rem(y + 2, heights) * 2 + core
    sibling = y * 2 + 1 - core
    following = lax.rem(me + 1, count)
    mine = pl.ds(me * share, share)

    def ring_peer(dx, k):
        side = 1 - 2 * lax.rem(k, 2)
        dz = rings // 2 + side * ((k + 1) // 2)
        return lax.rem(x + dx, planes) * rings + lax.rem(z + dz, rings)

    def far_first(k):
        return ring_peer(lax.rem(k // rings + 2, planes), lax.rem(k, rings))

    def near_first(k):
        return ring_peer(k // rings, lax.rem(k, rings))

    def each_peer(order, skip, step):
        def one(k, carry):
            step(order(k))
            return carry

        lax.fori_loop(0, skip, one, 0)
        lax.fori_loop(skip + 1, count, one, 0)

    last_of = {far_first: 2 * rings + rings - 1, near_first: rings - 1}

    def to_all(order, step):
        each_peer(order, last_of[order], step)

    barrier = pltpu.get_barrier_semaphore()

    def greet(to):
        pl.semaphore_signal(barrier, inc=1, device_id={"seq": to}, device_id_type=MESH)

    to_all(far_first, greet)
    for other in (down, up, sibling):
        pl.semaphore_signal(barrier, inc=1, device_id={"chan": other}, device_id_type=MESH)

    load_taps = pltpu.make_async_copy(taps_hbm, taps_ref, load_sem.at[3])
    load_taps.start()
    load_filt = pltpu.make_async_copy(filt_hbm, filt_ref, load_sem.at[4])
    load_filt.start()
    load_pair = pltpu.make_async_copy(proj_hbm.at[1:3], proj.at[1:3], load_sem.at[0])
    load_pair.start()
    load_query = pltpu.make_async_copy(proj_hbm.at[0], proj.at[0], load_sem.at[1])
    load_query.start()
    load_weight = pltpu.make_async_copy(weight_hbm, weight, load_sem.at[2])

    for h in range(2):
        product_in[h, 0:LANES, :] = jnp.zeros((LANES, LANES), jnp.bfloat16)

    def widen(s):
        for q in range(blocks):
            ext[s, q, pl.ds(PAD, rows), :] = proj[s, :, q * LANES : (q + 1) * LANES].astype(jnp.float32)

    def short(s, q, first, size):
        lanes = pl.ds(pl.multiple_of(q * LANES, LANES), LANES)
        taps = taps_ref[s, :, lanes]
        value = taps[0:1, :] * ext[s, q, pl.ds(first + PAD, size), :]
        for j in range(1, TAPS):
            value = value + taps[j : j + 1, :] * ext[s, q, pl.ds(first + PAD - j, size), :]
        return value

    def each_block(step):
        def one(q, carry):
            step(q)
            return carry

        lax.fori_loop(0, blocks, one, 0)

    def block_rows(q):
        return pl.ds(pl.multiple_of(q * LANES, LANES), LANES)

    def late_products(q):
        value = short(1, q, LANES, LANES) * short(2, q, LANES, LANES)
        product_out[1, block_rows(q), :] = value.T.astype(jnp.bfloat16)

    def early_products(q):
        early[q, 8:, :] = short(1, q, 8, LANES - 8) * short(2, q, 8, LANES - 8)

    def send_product(h, to):
        pltpu.make_async_remote_copy(
            src_ref=product_out.at[h, pl.ds(to * share, share), :],
            dst_ref=product_in.at[h, pl.ds(LANES + me * share, share), :],
            send_sem=product_send.at[0],
            recv_sem=product_recv.at[h],
            device_id={"seq": to},
            device_id_type=MESH,
        ).start()

    def keep_product(h):
        pltpu.make_async_copy(
            product_out.at[h, mine, :],
            product_in.at[h, pl.ds(LANES + me * share, share), :],
            product_recv.at[h],
        ).start()

    load_taps.wait()
    load_pair.wait()
    widen(1)
    widen(2)
    each_block(late_products)

    load_filt.wait()
    for g in range(groups):
        filt_mine[g] = filt_ref[g : g + 1, :]
    filt_all[0] = jnp.zeros(filt_all.shape[1:], jnp.float32)
    for q in range(blocks):
        edge = [ext[s, q, pl.ds(PAD + rows - 8, 8), :] for s in (1, 2)]
        edge_out[:, q * LANES : (q + 1) * LANES] = jnp.concatenate(edge, axis=0).astype(jnp.bfloat16)

    pl.semaphore_wait(barrier, count + 2)

    def halo_of(source, target, at):
        return pltpu.make_async_remote_copy(
            src_ref=source,
            dst_ref=target,
            send_sem=halo_sem.at[at],
            recv_sem=halo_sem.at[at + 1],
            device_id={"seq": following},
            device_id_type=MESH,
        )

    pair_halo = halo_of(edge_out, edge_in, 0)
    pair_halo.start()

    def send_filter(to):
        pltpu.make_async_remote_copy(
            src_ref=filt_mine.at[to // (count // groups)],
            dst_ref=filt_all.at[me + 1],
            send_sem=filt_sem.at[0],
            recv_sem=filt_sem.at[1],
            device_id={"seq": to},
            device_id_type=MESH,
        ).start()

    to_all(far_first, send_filter)
    pltpu.make_async_copy(
        filt_mine.at[me // (count // groups)], filt_all.at[me + 1], filt_sem.at[1]
    ).start()
    to_all(far_first, functools.partial(send_product, 1))
    keep_product(1)

    each_block(early_products)
    pair_halo.wait()
    for q in range(blocks):
        edge = edge_in[:, q * LANES : (q + 1) * LANES].astype(jnp.float32)
        edge = jnp.where(me == 0, 0.0, edge)
        ext[1, q, 8:PAD, :] = edge[0:8]
        ext[2, q, 8:PAD, :] = edge[8:]

    def first_products(q):
        early[q, 0:8, :] = short(1, q, 0, 8) * short(2, q, 0, 8)
        product_out[0, block_rows(q), :] = early[q].T.astype(jnp.bfloat16)

    for k in range(planes):
        dx = (k + 2) % planes
        first_products(lax.rem(x + dx, planes))

        def one(i, carry):
            send_product(0, ring_peer(dx, i))
            return carry

        lax.fori_loop(0, rings - 1 if dx == 0 else rings, one, 0)
        if dx == 0:
            keep_product(0)
    load_weight.start()

    query_halo = halo_of(proj.at[0, pl.ds(rows - PAD, PAD), :], halo, 2)
    load_query.wait()
    query_halo.start()
    widen(0)
    def spread(d):
        line = jnp.concatenate([filt_all[d][:, rows - LANES :], filt_all[d + 1]], axis=1)
        wide = jnp.broadcast_to(line, (LANES, line.shape[1]))
        value = pltpu.roll(wide, 0, 1, stride=1, stride_axis=0)[:, LANES:]
        top = value.astype(jnp.bfloat16)
        high[d] = top
        low[d] = (value - top.astype(jnp.float32)).astype(jnp.bfloat16)

    def lagged(table, d):
        before = table[d - 1][:, LANES:] if d else jnp.zeros((LANES, LANES), jnp.bfloat16)
        return jnp.concatenate([before, table[d][:, :LANES]], axis=1)

    def convolve_late(d):
        size = channels - share * d
        left = jnp.concatenate(
            [
                product_in[1, LANES : LANES + size, :],
                product_in[1, LANES - share : LANES - share + size, :],
            ],
            axis=1,
        )
        part = None
        for table in (high, low):
            right = jnp.concatenate([lagged(table, d), lagged(table, d + 1)], axis=0)
            more = jnp.dot(left, right, preferred_element_type=jnp.float32)
            part = more if part is None else part + more
        if d == 0:
            total[...] = part
        else:
            total[share * d :, :] += part

    def convolve_early(block):
        base = pl.multiple_of(block * LANES, LANES)

        def lags(step, value):
            for e in range(0, per_block, 2):
                d = step * per_block + e
                first = LANES + base - share * d
                left = jnp.concatenate(
                    [
                        product_in[0, pl.ds(pl.multiple_of(first, share), LANES), :],
                        product_in[0, pl.ds(pl.multiple_of(first - share, share), LANES), :],
                    ],
                    axis=1,
                )
                for table in (high,):
                    right = table[pl.ds(d, 2)].reshape(2 * LANES, rows)
                    value = value + jnp.dot(left, right, preferred_element_type=jnp.float32)
            return value

        value = lax.fori_loop(0, block + 1, lags, total[pl.ds(base, LANES), :])
        conv_out[pl.ds(base, LANES), :] = value.astype(jnp.bfloat16)

    pltpu.make_async_copy(
        filt_all.at[pl.ds(1, count)], filt_all.at[pl.ds(1, count)], filt_sem.at[1]
    ).wait()
    for d in range(count):
        spread(d)
    whole = product_in.at[1, pl.ds(LANES, channels), :]
    pltpu.make_async_copy(whole, whole, product_recv.at[1]).wait()
    for d in range(0, count, 2):
        convolve_late(d)
    query_halo.wait()
    for q in range(blocks):
        before = halo[:, q * LANES : (q + 1) * LANES].astype(jnp.float32)
        ext[0, q, 0:PAD, :] = jnp.where(me == 0, 0.0, before)

    def queries(q):
        for first in (0, LANES):
            query[q, first : first + LANES, :] = short(0, q, first, LANES)

    each_block(queries)

    whole = product_in.at[0, pl.ds(LANES, channels), :]
    pltpu.make_async_copy(whole, whole, product_recv.at[0]).wait()
    def send_back(to):
        pltpu.make_async_remote_copy(
            src_ref=conv_out.at[pl.ds(to * share, share), :],
            dst_ref=conv_in.at[mine, :],
            send_sem=conv_send.at[0],
            recv_sem=conv_recv.at[me // per_block],
            device_id={"seq": to},
            device_id_type=MESH,
        ).start()

    for dx in BACK_ORDER:
        convolve_early(lax.rem(x + dx, blocks))

        def one(i, carry):
            send_back(ring_peer(dx, i))
            return carry

        lax.fori_loop(0, rings - 1 if dx == 0 else rings, one, 0)
        if dx == 0:
            own = conv_recv.at[me // per_block]
            pltpu.make_async_copy(conv_out.at[mine], conv_in.at[mine], own).start()

    def pass_on(source, block, to):
        pltpu.make_async_remote_copy(
            src_ref=gated.at[source, block],
            dst_ref=gated.at[source, block],
            send_sem=gated_send.at[0],
            recv_sem=gated_recv.at[source, block],
            device_id={"chan": to},
            device_id_type=MESH,
        ).start()

    def arrived(source, block):
        slot = gated.at[source, block]
        pltpu.make_async_copy(slot, slot, gated_recv.at[source, block]).wait()

    def block_at(k):
        return lax.rem(x + blocks - BACK_ORDER[k], blocks)

    def gate(k):
        block = block_at(k)
        part = block_rows(block)
        pltpu.make_async_copy(conv_in.at[part], conv_in.at[part], conv_recv.at[block]).wait()
        value = conv_in[part, :].astype(jnp.float32).T
        gated[chan, block] = (value * query[block]).astype(jnp.bfloat16)
        for to in (down, sibling):
            pass_on(chan, block, to)

    def send_up(k):
        pass_on(chan, block_at(k), up)

    def near_up(k):
        block = block_at(k)
        arrived(up, block)
        pass_on(up, block, down)
        pass_on(up, block, sibling)

    def near_down(k):
        block = block_at(k)
        arrived(down, block)
        pass_on(down, block, sibling)

    def relay_far(k):
        block = block_at(k)
        arrived(far, block)
        pass_on(far, block, sibling)

    def project_part(k, sources):
        block = block_at(k)
        left = jnp.concatenate([gated[c, block] for c in sources], axis=1)
        right = jnp.concatenate(
            [
                weight[pl.ds(pl.multiple_of(c * channels + block * LANES, LANES), LANES), :]
                for c in sources
            ],
            axis=0,
        )
        return jnp.dot(left, right, preferred_element_type=jnp.float32)

    own_stream = (chan, up, down, far)
    other_stream = [c + 1 - 2 * core for c in own_stream]

    def project_mine(k):
        part = project_part(k, own_stream)
        if k == 0:
            out_total[...] = part
        else:
            out_total[...] += part

    def project_other(k):
        for c in other_stream:
            arrived(c, block_at(k))
        out_total[...] += project_part(k, other_stream)

    def project_near(k):
        for c in other_stream[:3]:
            arrived(c, block_at(k))
        out_total[...] += project_part(k, own_stream[:3] + tuple(other_stream[:3]))

    def project_rest(k):
        arrived(other_stream[3], block_at(k))
        part = project_part(k, (far, other_stream[3]))
        out_ref[...] = (out_total[...] + part).astype(jnp.bfloat16)

    load_weight.wait()
    steps = (
        (gate, 0), (send_up, 0), (gate, 1), (send_up, 1), (gate, 2),
        (send_up, 2), (gate, 3), (send_up, 3), (near_up, 0), (near_up, 1),
        (near_up, 2), (near_up, 3), (near_down, 0), (near_down, 1), (near_down, 2),
        (near_down, 3), (relay_far, 0), (relay_far, 1), (project_mine, 0), (project_other, 0),
        (relay_far, 2), (project_mine, 1), (project_other, 1), (project_mine, 2), (relay_far, 3),
        (project_other, 2), (project_near, 3), (project_rest, 3),
    )
    for step, k in steps:
        step(k)

    sent = product_out.at[0:2, pl.ds(0, (count - 1) * share), :]
    pltpu.make_async_copy(sent, sent, product_send.at[0]).wait()
    sent = conv_out.at[pl.ds(0, (count - 1) * share), :]
    pltpu.make_async_copy(sent, sent, conv_send.at[0]).wait()
    sent = filt_all.at[pl.ds(1, count - 1)]
    pltpu.make_async_copy(sent, sent, filt_sem.at[0]).wait()
    sent = gated.at[pl.ds(0, 7)]
    pltpu.make_async_copy(sent, sent, gated_send.at[0]).wait()


def solution(mesh):
    count = mesh.shape["seq"]
    chans = mesh.shape["chan"]
    planes, rings = 4, count // 4

    def per_device(projections, short_taps, filters, out_weight):
        rows, channels = projections.shape[1], projections.shape[2]
        blocks = channels // LANES
        share = channels // count
        vmem = pl.BlockSpec(memory_space=pltpu.VMEM)
        hbm = pl.BlockSpec(memory_space=pl.ANY)
        bf16, f32 = jnp.bfloat16, jnp.float32
        dma = pltpu.SemaphoreType.DMA
        return pl.pallas_call(
            functools.partial(kernel, (count, planes, rings)),
            out_shape=jax.ShapeDtypeStruct((rows, out_weight.shape[1]), bf16),
            in_specs=[hbm, hbm, hbm, hbm],
            out_specs=vmem,
            scratch_shapes=[
                pltpu.VMEM(short_taps.shape, f32),
                pltpu.VMEM(filters.shape, f32),
                pltpu.VMEM(projections.shape, bf16),
                pltpu.VMEM((PAD, channels), bf16),
                pltpu.VMEM((PAD, channels), bf16),
                pltpu.VMEM((PAD, channels), bf16),
                pltpu.VMEM((3, blocks, PAD + rows, LANES), f32),
                pltpu.VMEM((filters.shape[0], 1, rows), f32),
                pltpu.VMEM((count + 1, 1, rows), f32),
                pltpu.VMEM((count, LANES, rows), bf16),
                pltpu.VMEM((count, LANES, rows), bf16),
                pltpu.VMEM((blocks, LANES, LANES), f32),
                pltpu.VMEM((2, channels, LANES), bf16),
                pltpu.VMEM((2, LANES + channels, LANES), bf16),
                pltpu.VMEM((channels, rows), f32),
                pltpu.VMEM((channels, rows), bf16),
                pltpu.VMEM((channels, rows), bf16),
                pltpu.VMEM((blocks, rows, LANES), f32),
                pltpu.VMEM((chans, blocks, rows, LANES), bf16),
                pltpu.VMEM(out_weight.shape, bf16),
                pltpu.VMEM((rows, out_weight.shape[1]), f32),
                dma((5,)),
                dma((4,)),
                dma((2,)),
                dma((1,)),
                dma((2,)),
                dma((1,)),
                dma((blocks,)),
                dma((1,)),
                dma((chans, blocks)),
            ],
            compiler_params=pltpu.CompilerParams(
                collective_id=0, has_side_effects=True, vmem_limit_bytes=24 * 2**20
            ),
        )(*[pltpu.with_memory_space_constraint(a, pltpu.HBM) for a in (projections, short_taps, filters, out_weight)])

    return jax.shard_map(
        per_device,
        mesh=mesh,
        in_specs=(P(None, "seq", "chan"), P(None, None, "chan"), P("chan", "seq"), P(None, "chan")),
        out_specs=P("seq", "chan"),
        check_vma=False,
    )
```

```python
import functools

import jax
import jax.numpy as jnp
from jax import lax
from jax.experimental import pallas as pl
from jax.experimental.pallas import tpu as pltpu
from jax.sharding import PartitionSpec as P

MESH = pl.DeviceIdType.MESH
TAPS = 7
EARLY_ORDER = (2, 3, 1, 0)
BACK_ORDER = (0, 2, 1, 3)
PAD = 16
LANES = 128


def kernel(
    sizes,
    proj_hbm,
    taps_hbm,
    filt_hbm,
    weight_hbm,
    out_ref,
    taps_ref,
    filt_ref,
    proj,
    halo,
    edge_out,
    edge_in,
    ext,
    filt_mine,
    filt_all,
    high,
    low,
    early,
    product_out,
    product_in,
    total,
    conv_out,
    conv_in,
    query,
    gated,
    weight,
    out_total,
    load_sem,
    halo_sem,
    filt_sem,
    product_send,
    product_recv,
    conv_send,
    conv_recv,
    gated_send,
    gated_recv,
):
    count, planes, rings = sizes
    rows = proj.shape[1]
    channels = proj.shape[2]
    share = channels // count
    blocks = channels // LANES
    per_block = count // blocks
    groups = filt_ref.shape[0]
    me = lax.axis_index("seq")
    chan = lax.axis_index("chan")
    x, z = me // rings, lax.rem(me, rings)
    y, core = chan // 2, lax.rem(chan, 2)
    heights = lax.axis_size("chan") // 2
    step_up = 1 - 2 * core
    down = lax.rem(y + step_up + heights, heights) * 2 + core
    up = lax.rem(y - step_up + heights, heights) * 2 + core
    far = lax.rem(y + 2, heights) * 2 + core
    sibling = y * 2 + 1 - core
    following = lax.rem(me + 1, count)
    mine = pl.ds(me * share, share)

    def ring_peer(dx, k):
        side = 1 - 2 * lax.rem(k, 2)
        dz = rings // 2 + side * ((k + 1) // 2)
        return lax.rem(x + dx, planes) * rings + lax.rem(z + dz, rings)

    def far_first(k):
        return ring_peer(lax.rem(k // rings + 2, planes), lax.rem(k, rings))

    def near_first(k):
        return ring_peer(k // rings, lax.rem(k, rings))

    def each_peer(order, skip, step):
        def one(k, carry):
            step(order(k))
            return carry

        lax.fori_loop(0, skip, one, 0)
        lax.fori_loop(skip + 1, count, one, 0)

    last_of = {far_first: 2 * rings + rings - 1, near_first: rings - 1}

    def to_all(order, step):
        each_peer(order, last_of[order], step)

    barrier = pltpu.get_barrier_semaphore()

    def greet(to):
        pl.semaphore_signal(barrier, inc=1, device_id={"seq": to}, device_id_type=MESH)

    to_all(far_first, greet)
    for other in (down, up, sibling):
        pl.semaphore_signal(barrier, inc=1, device_id={"chan": other}, device_id_type=MESH)

    load_taps = pltpu.make_async_copy(taps_hbm, taps_ref, load_sem.at[3])
    load_taps.start()
    load_filt = pltpu.make_async_copy(filt_hbm, filt_ref, load_sem.at[4])
    load_filt.start()
    load_pair = pltpu.make_async_copy(proj_hbm.at[1:3], proj.at[1:3], load_sem.at[0])
    load_pair.start()
    load_query = pltpu.make_async_copy(proj_hbm.at[0], proj.at[0], load_sem.at[1])
    load_query.start()
    load_weight = pltpu.make_async_copy(weight_hbm, weight, load_sem.at[2])

    for h in range(2):
        product_in[h, 0:LANES, :] = jnp.zeros((LANES, LANES), jnp.bfloat16)

    def widen(s):
        for q in range(blocks):
            ext[s, q, pl.ds(PAD, rows), :] = proj[s, :, q * LANES : (q + 1) * LANES].astype(jnp.float32)

    def short(s, q, first, size):
        lanes = pl.ds(pl.multiple_of(q * LANES, LANES), LANES)
        taps = taps_ref[s, :, lanes]
        value = taps[0:1, :] * ext[s, q, pl.ds(first + PAD, size), :]
        for j in range(1, TAPS):
            value = value + taps[j : j + 1, :] * ext[s, q, pl.ds(first + PAD - j, size), :]
        return value

    def each_block(step):
        def one(q, carry):
            step(q)
            return carry

        lax.fori_loop(0, blocks, one, 0)

    def block_rows(q):
        return pl.ds(pl.multiple_of(q * LANES, LANES), LANES)

    def late_products(q):
        value = short(1, q, LANES, LANES) * short(2, q, LANES, LANES)
        product_out[1, block_rows(q), :] = value.T.astype(jnp.bfloat16)

    def early_products(q):
        early[q, 8:, :] = short(1, q, 8, LANES - 8) * short(2, q, 8, LANES - 8)

    def send_product(h, to):
        pltpu.make_async_remote_copy(
            src_ref=product_out.at[h, pl.ds(to * share, share), :],
            dst_ref=product_in.at[h, pl.ds(LANES + me * share, share), :],
            send_sem=product_send.at[0],
            recv_sem=product_recv.at[blocks if h else x],
            device_id={"seq": to},
            device_id_type=MESH,
        ).start()

    def keep_product(h):
        pltpu.make_async_copy(
            product_out.at[h, mine, :],
            product_in.at[h, pl.ds(LANES + me * share, share), :],
            product_recv.at[blocks if h else x],
        ).start()

    load_taps.wait()
    load_pair.wait()
    widen(1)
    widen(2)
    each_block(late_products)

    load_filt.wait()
    for g in range(groups):
        filt_mine[g] = filt_ref[g : g + 1, :]
    filt_all[0] = jnp.zeros(filt_all.shape[1:], jnp.float32)
    for q in range(blocks):
        edge = [ext[s, q, pl.ds(PAD + rows - 8, 8), :] for s in (1, 2)]
        edge_out[:, q * LANES : (q + 1) * LANES] = jnp.concatenate(edge, axis=0).astype(jnp.bfloat16)

    pl.semaphore_wait(barrier, count + 2)

    def halo_of(source, target, at):
        return pltpu.make_async_remote_copy(
            src_ref=source,
            dst_ref=target,
            send_sem=halo_sem.at[at],
            recv_sem=halo_sem.at[at + 1],
            device_id={"seq": following},
            device_id_type=MESH,
        )

    pair_halo = halo_of(edge_out, edge_in, 0)
    pair_halo.start()

    def send_filter(to):
        pltpu.make_async_remote_copy(
            src_ref=filt_mine.at[to // (count // groups)],
            dst_ref=filt_all.at[me + 1],
            send_sem=filt_sem.at[0],
            recv_sem=filt_sem.at[1],
            device_id={"seq": to},
            device_id_type=MESH,
        ).start()

    to_all(far_first, send_filter)
    pltpu.make_async_copy(
        filt_mine.at[me // (count // groups)], filt_all.at[me + 1], filt_sem.at[1]
    ).start()
    to_all(far_first, functools.partial(send_product, 1))
    keep_product(1)

    each_block(early_products)
    pair_halo.wait()
    for q in range(blocks):
        edge = edge_in[:, q * LANES : (q + 1) * LANES].astype(jnp.float32)
        edge = jnp.where(me == 0, 0.0, edge)
        ext[1, q, 8:PAD, :] = edge[0:8]
        ext[2, q, 8:PAD, :] = edge[8:]

    def first_products(q):
        early[q, 0:8, :] = short(1, q, 0, 8) * short(2, q, 0, 8)
        product_out[0, block_rows(q), :] = early[q].T.astype(jnp.bfloat16)

    for dx in EARLY_ORDER:
        first_products(lax.rem(x + dx, planes))

        def one(i, carry):
            send_product(0, ring_peer(dx, i))
            return carry

        lax.fori_loop(0, rings - 1 if dx == 0 else rings, one, 0)
        if dx == 0:
            keep_product(0)
    load_weight.start()

    query_halo = halo_of(proj.at[0, pl.ds(rows - PAD, PAD), :], halo, 2)
    load_query.wait()
    query_halo.start()
    widen(0)
    def spread(d):
        line = jnp.concatenate([filt_all[d][:, rows - LANES :], filt_all[d + 1]], axis=1)
        wide = jnp.broadcast_to(line, (LANES, line.shape[1]))
        value = pltpu.roll(wide, 0, 1, stride=1, stride_axis=0)[:, LANES:]
        top = value.astype(jnp.bfloat16)
        high[d] = top
        low[d] = (value - top.astype(jnp.float32)).astype(jnp.bfloat16)

    def lagged(table, d):
        before = table[d - 1][:, LANES:] if d else jnp.zeros((LANES, LANES), jnp.bfloat16)
        return jnp.concatenate([before, table[d][:, :LANES]], axis=1)

    def convolve_late(d):
        size = channels - share * d
        left = jnp.concatenate(
            [
                product_in[1, LANES : LANES + size, :],
                product_in[1, LANES - share : LANES - share + size, :],
            ],
            axis=1,
        )
        part = None
        for table in (high, low):
            right = jnp.concatenate([lagged(table, d), lagged(table, d + 1)], axis=0)
            more = jnp.dot(left, right, preferred_element_type=jnp.float32)
            part = more if part is None else part + more
        if d == 0:
            total[...] = part
        else:
            total[share * d :, :] += part

    def early_arrived(dx):
        source = lax.rem(x + blocks - dx, blocks)
        place = product_in.at[0, pl.ds(pl.multiple_of((source + 1) * LANES, LANES), LANES), :]
        pltpu.make_async_copy(place, place, product_recv.at[source]).wait()

    def convolve_early(block, parts=None):
        base = pl.multiple_of(block * LANES, LANES)

        def lags(step, value):
            for e in range(0, per_block, 2):
                d = step * per_block + e
                first = LANES + base - share * d
                left = jnp.concatenate(
                    [
                        product_in[0, pl.ds(pl.multiple_of(first, share), LANES), :],
                        product_in[0, pl.ds(pl.multiple_of(first - share, share), LANES), :],
                    ],
                    axis=1,
                )
                for table in (high,):
                    right = table[pl.ds(d, 2)].reshape(2 * LANES, rows)
                    value = value + jnp.dot(left, right, preferred_element_type=jnp.float32)
            return value

        value = total[pl.ds(base, LANES), :]
        if parts is None:
            value = lax.fori_loop(0, block + 1, lags, value)
        else:
            for sources, steps in parts:
                for dx in sources:
                    early_arrived(dx)
                for step in steps:
                    stop = step + (block + blocks - step) // blocks
                    value = lax.fori_loop(step, stop, lags, value)
        conv_out[pl.ds(base, LANES), :] = value.astype(jnp.bfloat16)

    pltpu.make_async_copy(
        filt_all.at[pl.ds(1, count)], filt_all.at[pl.ds(1, count)], filt_sem.at[1]
    ).wait()
    for d in range(count):
        spread(d)
    whole = product_in.at[1, pl.ds(LANES, channels), :]
    pltpu.make_async_copy(whole, whole, product_recv.at[blocks]).wait()
    for d in range(0, count, 2):
        convolve_late(d)
    query_halo.wait()
    for q in range(blocks):
        before = halo[:, q * LANES : (q + 1) * LANES].astype(jnp.float32)
        ext[0, q, 0:PAD, :] = jnp.where(me == 0, 0.0, before)

    def queries(q):
        for first in (0, LANES):
            query[q, first : first + LANES, :] = short(0, q, first, LANES)

    each_block(queries)

    def send_back(to):
        pltpu.make_async_remote_copy(
            src_ref=conv_out.at[pl.ds(to * share, share), :],
            dst_ref=conv_in.at[mine, :],
            send_sem=conv_send.at[0],
            recv_sem=conv_recv.at[me // per_block],
            device_id={"seq": to},
            device_id_type=MESH,
        ).start()

    for dx in BACK_ORDER:
        if dx == 0:
            convolve_early(x, (((2, 3), (2, 3)), ((1,), (1,)), ((0,), (0,))))
        else:
            convolve_early(lax.rem(x + dx, blocks))

        def one(i, carry):
            send_back(ring_peer(dx, i))
            return carry

        lax.fori_loop(0, rings - 1 if dx == 0 else rings, one, 0)
        if dx == 0:
            own = conv_recv.at[me // per_block]
            pltpu.make_async_copy(conv_out.at[mine], conv_in.at[mine], own).start()

    def pass_on(source, block, to):
        pltpu.make_async_remote_copy(
            src_ref=gated.at[source, block],
            dst_ref=gated.at[source, block],
            send_sem=gated_send.at[0],
            recv_sem=gated_recv.at[source, block],
            device_id={"chan": to},
            device_id_type=MESH,
        ).start()

    def arrived(source, block):
        slot = gated.at[source, block]
        pltpu.make_async_copy(slot, slot, gated_recv.at[source, block]).wait()

    def block_at(k):
        return lax.rem(x + blocks - BACK_ORDER[k], blocks)

    def gate(k):
        block = block_at(k)
        part = block_rows(block)
        pltpu.make_async_copy(conv_in.at[part], conv_in.at[part], conv_recv.at[block]).wait()
        value = conv_in[part, :].astype(jnp.float32).T
        gated[chan, block] = (value * query[block]).astype(jnp.bfloat16)
        for to in (down, sibling):
            pass_on(chan, block, to)

    def send_up(k):
        pass_on(chan, block_at(k), up)

    def near_up(k):
        block = block_at(k)
        arrived(up, block)
        pass_on(up, block, down)
        pass_on(up, block, sibling)

    def near_down(k):
        block = block_at(k)
        arrived(down, block)
        pass_on(down, block, sibling)

    def relay_far(k):
        block = block_at(k)
        arrived(far, block)
        pass_on(far, block, sibling)

    def project_part(k, sources):
        block = block_at(k)
        left = jnp.concatenate([gated[c, block] for c in sources], axis=1)
        right = jnp.concatenate(
            [
                weight[pl.ds(pl.multiple_of(c * channels + block * LANES, LANES), LANES), :]
                for c in sources
            ],
            axis=0,
        )
        return jnp.dot(left, right, preferred_element_type=jnp.float32)

    own_stream = (chan, up, down, far)
    other_stream = [c + 1 - 2 * core for c in own_stream]

    def project_mine(k):
        part = project_part(k, own_stream)
        if k == 0:
            out_total[...] = part
        else:
            out_total[...] += part

    def project_other(k):
        for c in other_stream:
            arrived(c, block_at(k))
        out_total[...] += project_part(k, other_stream)

    def project_near(k):
        for c in other_stream[:3]:
            arrived(c, block_at(k))
        out_total[...] += project_part(k, own_stream[:3] + tuple(other_stream[:3]))

    def project_rest(k):
        arrived(other_stream[3], block_at(k))
        part = project_part(k, (far, other_stream[3]))
        out_ref[...] = (out_total[...] + part).astype(jnp.bfloat16)

    load_weight.wait()
    steps = (
        (gate, 0), (send_up, 0), (gate, 1), (send_up, 1), (gate, 2),
        (send_up, 2), (gate, 3), (send_up, 3), (near_up, 0), (near_up, 1),
        (near_up, 2), (near_up, 3), (near_down, 0), (near_down, 1), (near_down, 2),
        (near_down, 3), (relay_far, 0), (relay_far, 1), (project_mine, 0), (project_other, 0),
        (relay_far, 2), (project_mine, 1), (project_other, 1), (project_mine, 2), (relay_far, 3),
        (project_other, 2), (project_near, 3), (project_rest, 3),
    )
    for step, k in steps:
        step(k)

    sent = product_out.at[0:2, pl.ds(0, (count - 1) * share), :]
    pltpu.make_async_copy(sent, sent, product_send.at[0]).wait()
    sent = conv_out.at[pl.ds(0, (count - 1) * share), :]
    pltpu.make_async_copy(sent, sent, conv_send.at[0]).wait()
    sent = filt_all.at[pl.ds(1, count - 1)]
    pltpu.make_async_copy(sent, sent, filt_sem.at[0]).wait()
    sent = gated.at[pl.ds(0, 7)]
    pltpu.make_async_copy(sent, sent, gated_send.at[0]).wait()


def solution(mesh):
    count = mesh.shape["seq"]
    chans = mesh.shape["chan"]
    planes, rings = 4, count // 4

    def per_device(projections, short_taps, filters, out_weight):
        rows, channels = projections.shape[1], projections.shape[2]
        blocks = channels // LANES
        share = channels // count
        vmem = pl.BlockSpec(memory_space=pltpu.VMEM)
        hbm = pl.BlockSpec(memory_space=pl.ANY)
        bf16, f32 = jnp.bfloat16, jnp.float32
        dma = pltpu.SemaphoreType.DMA
        return pl.pallas_call(
            functools.partial(kernel, (count, planes, rings)),
            out_shape=jax.ShapeDtypeStruct((rows, out_weight.shape[1]), bf16),
            in_specs=[hbm, hbm, hbm, hbm],
            out_specs=vmem,
            scratch_shapes=[
                pltpu.VMEM(short_taps.shape, f32),
                pltpu.VMEM(filters.shape, f32),
                pltpu.VMEM(projections.shape, bf16),
                pltpu.VMEM((PAD, channels), bf16),
                pltpu.VMEM((PAD, channels), bf16),
                pltpu.VMEM((PAD, channels), bf16),
                pltpu.VMEM((3, blocks, PAD + rows, LANES), f32),
                pltpu.VMEM((filters.shape[0], 1, rows), f32),
                pltpu.VMEM((count + 1, 1, rows), f32),
                pltpu.VMEM((count, LANES, rows), bf16),
                pltpu.VMEM((count, LANES, rows), bf16),
                pltpu.VMEM((blocks, LANES, LANES), f32),
                pltpu.VMEM((2, channels, LANES), bf16),
                pltpu.VMEM((2, LANES + channels, LANES), bf16),
                pltpu.VMEM((channels, rows), f32),
                pltpu.VMEM((channels, rows), bf16),
                pltpu.VMEM((channels, rows), bf16),
                pltpu.VMEM((blocks, rows, LANES), f32),
                pltpu.VMEM((chans, blocks, rows, LANES), bf16),
                pltpu.VMEM(out_weight.shape, bf16),
                pltpu.VMEM((rows, out_weight.shape[1]), f32),
                dma((5,)),
                dma((4,)),
                dma((2,)),
                dma((1,)),
                dma((blocks + 1,)),
                dma((1,)),
                dma((blocks,)),
                dma((1,)),
                dma((chans, blocks)),
            ],
            compiler_params=pltpu.CompilerParams(
                collective_id=0, has_side_effects=True, vmem_limit_bytes=24 * 2**20
            ),
        )(*[pltpu.with_memory_space_constraint(a, pltpu.HBM) for a in (projections, short_taps, filters, out_weight)])

    return jax.shard_map(
        per_device,
        mesh=mesh,
        in_specs=(P(None, "seq", "chan"), P(None, None, "chan"), P("chan", "seq"), P(None, "chan")),
        out_specs=P("seq", "chan"),
        check_vma=False,
    )
```

```python
import functools

import jax
import jax.numpy as jnp
from jax import lax
from jax.experimental import pallas as pl
from jax.experimental.pallas import tpu as pltpu
from jax.sharding import PartitionSpec as P

MESH = pl.DeviceIdType.MESH
TAPS = 7
EARLY_ORDER = (2, 3, 1, 0)
BACK_ORDER = (0, 2, 1, 3)
PAD = 16
LANES = 128


def kernel(
    sizes,
    proj_hbm,
    taps_hbm,
    filt_hbm,
    weight_hbm,
    out_ref,
    taps_ref,
    filt_ref,
    proj,
    halo,
    edge_out,
    edge_in,
    ext,
    filt_mine,
    filt_all,
    high,
    low,
    early,
    product_out,
    product_in,
    total,
    conv_out,
    conv_in,
    query,
    gated,
    weight,
    out_total,
    load_sem,
    halo_sem,
    filt_sem,
    product_send,
    product_recv,
    conv_send,
    conv_recv,
    gated_send,
    gated_recv,
):
    count, planes, rings = sizes
    rows = proj.shape[1]
    channels = proj.shape[2]
    share = channels // count
    blocks = channels // LANES
    per_block = count // blocks
    groups = filt_ref.shape[0]
    me = lax.axis_index("seq")
    chan = lax.axis_index("chan")
    x, z = me // rings, lax.rem(me, rings)
    y, core = chan // 2, lax.rem(chan, 2)
    heights = lax.axis_size("chan") // 2
    step_up = 1 - 2 * core
    down = lax.rem(y + step_up + heights, heights) * 2 + core
    up = lax.rem(y - step_up + heights, heights) * 2 + core
    far = lax.rem(y + 2, heights) * 2 + core
    sibling = y * 2 + 1 - core
    following = lax.rem(me + 1, count)
    mine = pl.ds(me * share, share)

    def ring_peer(dx, k):
        side = 1 - 2 * lax.rem(k, 2)
        dz = rings // 2 + side * ((k + 1) // 2)
        return lax.rem(x + dx, planes) * rings + lax.rem(z + dz, rings)

    def far_first(k):
        return ring_peer(lax.rem(k // rings + 2, planes), lax.rem(k, rings))

    def near_first(k):
        return ring_peer(k // rings, lax.rem(k, rings))

    def each_peer(order, skip, step):
        def one(k, carry):
            step(order(k))
            return carry

        lax.fori_loop(0, skip, one, 0)
        lax.fori_loop(skip + 1, count, one, 0)

    last_of = {far_first: 2 * rings + rings - 1, near_first: rings - 1}

    def to_all(order, step):
        each_peer(order, last_of[order], step)

    barrier = pltpu.get_barrier_semaphore()

    def greet(to):
        pl.semaphore_signal(barrier, inc=1, device_id={"seq": to}, device_id_type=MESH)

    to_all(far_first, greet)
    for other in (down, up, far, sibling):
        pl.semaphore_signal(barrier, inc=1, device_id={"chan": other}, device_id_type=MESH)

    load_taps = pltpu.make_async_copy(taps_hbm, taps_ref, load_sem.at[3])
    load_taps.start()
    load_filt = pltpu.make_async_copy(filt_hbm, filt_ref, load_sem.at[4])
    load_filt.start()
    load_pair = pltpu.make_async_copy(proj_hbm.at[1:3], proj.at[1:3], load_sem.at[0])
    load_pair.start()
    load_query = pltpu.make_async_copy(proj_hbm.at[0], proj.at[0], load_sem.at[1])
    load_query.start()
    load_weight = pltpu.make_async_copy(weight_hbm, weight, load_sem.at[2])

    for h in range(2):
        product_in[h, 0:LANES, :] = jnp.zeros((LANES, LANES), jnp.bfloat16)

    def widen(s):
        for q in range(blocks):
            ext[s, q, pl.ds(PAD, rows), :] = proj[s, :, q * LANES : (q + 1) * LANES].astype(jnp.float32)

    def short(s, q, first, size):
        lanes = pl.ds(pl.multiple_of(q * LANES, LANES), LANES)
        taps = taps_ref[s, :, lanes]
        value = taps[0:1, :] * ext[s, q, pl.ds(first + PAD, size), :]
        for j in range(1, TAPS):
            value = value + taps[j : j + 1, :] * ext[s, q, pl.ds(first + PAD - j, size), :]
        return value

    def each_block(step):
        def one(q, carry):
            step(q)
            return carry

        lax.fori_loop(0, blocks, one, 0)

    def block_rows(q):
        return pl.ds(pl.multiple_of(q * LANES, LANES), LANES)

    def late_products(q):
        value = short(1, q, LANES, LANES) * short(2, q, LANES, LANES)
        product_out[1, block_rows(q), :] = value.T.astype(jnp.bfloat16)

    def early_products(q):
        early[q, 8:, :] = short(1, q, 8, LANES - 8) * short(2, q, 8, LANES - 8)

    def send_product(h, to):
        pltpu.make_async_remote_copy(
            src_ref=product_out.at[h, pl.ds(to * share, share), :],
            dst_ref=product_in.at[h, pl.ds(LANES + me * share, share), :],
            send_sem=product_send.at[0],
            recv_sem=product_recv.at[blocks if h else x],
            device_id={"seq": to},
            device_id_type=MESH,
        ).start()

    def keep_product(h):
        pltpu.make_async_copy(
            product_out.at[h, mine, :],
            product_in.at[h, pl.ds(LANES + me * share, share), :],
            product_recv.at[blocks if h else x],
        ).start()

    load_taps.wait()
    load_pair.wait()
    widen(1)
    widen(2)
    each_block(late_products)

    load_filt.wait()
    for g in range(groups):
        filt_mine[g] = filt_ref[g : g + 1, :]
    filt_all[0] = jnp.zeros(filt_all.shape[1:], jnp.float32)
    for q in range(blocks):
        edge = [ext[s, q, pl.ds(PAD + rows - 8, 8), :] for s in (1, 2)]
        edge_out[:, q * LANES : (q + 1) * LANES] = jnp.concatenate(edge, axis=0).astype(jnp.bfloat16)

    pl.semaphore_wait(barrier, count + 3)

    def halo_of(source, target, at):
        return pltpu.make_async_remote_copy(
            src_ref=source,
            dst_ref=target,
            send_sem=halo_sem.at[at],
            recv_sem=halo_sem.at[at + 1],
            device_id={"seq": following},
            device_id_type=MESH,
        )

    pair_halo = halo_of(edge_out, edge_in, 0)
    pair_halo.start()

    def send_filter(to):
        pltpu.make_async_remote_copy(
            src_ref=filt_mine.at[to // (count // groups)],
            dst_ref=filt_all.at[me + 1],
            send_sem=filt_sem.at[0],
            recv_sem=filt_sem.at[1],
            device_id={"seq": to},
            device_id_type=MESH,
        ).start()

    to_all(far_first, send_filter)
    pltpu.make_async_copy(
        filt_mine.at[me // (count // groups)], filt_all.at[me + 1], filt_sem.at[1]
    ).start()
    to_all(far_first, functools.partial(send_product, 1))
    keep_product(1)

    each_block(early_products)
    pair_halo.wait()
    for q in range(blocks):
        edge = edge_in[:, q * LANES : (q + 1) * LANES].astype(jnp.float32)
        edge = jnp.where(me == 0, 0.0, edge)
        ext[1, q, 8:PAD, :] = edge[0:8]
        ext[2, q, 8:PAD, :] = edge[8:]

    def first_products(q):
        early[q, 0:8, :] = short(1, q, 0, 8) * short(2, q, 0, 8)
        product_out[0, block_rows(q), :] = early[q].T.astype(jnp.bfloat16)

    for dx in EARLY_ORDER:
        first_products(lax.rem(x + dx, planes))

        def one(i, carry):
            send_product(0, ring_peer(dx, i))
            return carry

        lax.fori_loop(0, rings - 1 if dx == 0 else rings, one, 0)
        if dx == 0:
            keep_product(0)
    load_weight.start()

    query_halo = halo_of(proj.at[0, pl.ds(rows - PAD, PAD), :], halo, 2)
    load_query.wait()
    query_halo.start()
    widen(0)
    def spread(d):
        line = jnp.concatenate([filt_all[d][:, rows - LANES :], filt_all[d + 1]], axis=1)
        wide = jnp.broadcast_to(line, (LANES, line.shape[1]))
        value = pltpu.roll(wide, 0, 1, stride=1, stride_axis=0)[:, LANES:]
        top = value.astype(jnp.bfloat16)
        high[d] = top
        low[d] = (value - top.astype(jnp.float32)).astype(jnp.bfloat16)

    def lagged(table, d):
        before = table[d - 1][:, LANES:] if d else jnp.zeros((LANES, LANES), jnp.bfloat16)
        return jnp.concatenate([before, table[d][:, :LANES]], axis=1)

    def convolve_late(d):
        size = channels - share * d
        left = jnp.concatenate(
            [
                product_in[1, LANES : LANES + size, :],
                product_in[1, LANES - share : LANES - share + size, :],
            ],
            axis=1,
        )
        part = None
        for table in (high, low):
            right = jnp.concatenate([lagged(table, d), lagged(table, d + 1)], axis=0)
            more = jnp.dot(left, right, preferred_element_type=jnp.float32)
            part = more if part is None else part + more
        if d == 0:
            total[...] = part
        else:
            total[share * d :, :] += part

    def early_arrived(dx):
        source = lax.rem(x + blocks - dx, blocks)
        place = product_in.at[0, pl.ds(pl.multiple_of((source + 1) * LANES, LANES), LANES), :]
        pltpu.make_async_copy(place, place, product_recv.at[source]).wait()

    def convolve_early(block, parts=None):
        base = pl.multiple_of(block * LANES, LANES)

        def lags(step, value):
            for e in range(0, per_block, 2):
                d = step * per_block + e
                first = LANES + base - share * d
                left = jnp.concatenate(
                    [
                        product_in[0, pl.ds(pl.multiple_of(first, share), LANES), :],
                        product_in[0, pl.ds(pl.multiple_of(first - share, share), LANES), :],
                    ],
                    axis=1,
                )
                for table in (high,):
                    right = table[pl.ds(d, 2)].reshape(2 * LANES, rows)
                    value = value + jnp.dot(left, right, preferred_element_type=jnp.float32)
            return value

        value = total[pl.ds(base, LANES), :]
        if parts is None:
            value = lax.fori_loop(0, block + 1, lags, value)
        else:
            for sources, steps in parts:
                for dx in sources:
                    early_arrived(dx)
                for step in steps:
                    stop = step + (block + blocks - step) // blocks
                    value = lax.fori_loop(step, stop, lags, value)
        conv_out[pl.ds(base, LANES), :] = value.astype(jnp.bfloat16)

    pltpu.make_async_copy(
        filt_all.at[pl.ds(1, count)], filt_all.at[pl.ds(1, count)], filt_sem.at[1]
    ).wait()
    for d in range(count):
        spread(d)
    whole = product_in.at[1, pl.ds(LANES, channels), :]
    pltpu.make_async_copy(whole, whole, product_recv.at[blocks]).wait()
    for d in range(0, count, 2):
        convolve_late(d)
    query_halo.wait()
    for q in range(blocks):
        before = halo[:, q * LANES : (q + 1) * LANES].astype(jnp.float32)
        ext[0, q, 0:PAD, :] = jnp.where(me == 0, 0.0, before)

    def queries(q):
        for first in (0, LANES):
            query[q, first : first + LANES, :] = short(0, q, first, LANES)

    each_block(queries)

    def send_back(to):
        pltpu.make_async_remote_copy(
            src_ref=conv_out.at[pl.ds(to * share, share), :],
            dst_ref=conv_in.at[mine, :],
            send_sem=conv_send.at[0],
            recv_sem=conv_recv.at[me // per_block],
            device_id={"seq": to},
            device_id_type=MESH,
        ).start()

    for dx in BACK_ORDER:
        if dx == 0:
            convolve_early(x, (((2, 3), (2, 3)), ((1,), (1,)), ((0,), (0,))))
        else:
            convolve_early(lax.rem(x + dx, blocks))

        def one(i, carry):
            send_back(ring_peer(dx, i))
            return carry

        lax.fori_loop(0, rings - 1 if dx == 0 else rings, one, 0)
        if dx == 0:
            own = conv_recv.at[me // per_block]
            pltpu.make_async_copy(conv_out.at[mine], conv_in.at[mine], own).start()

    def pass_on(source, block, to):
        pltpu.make_async_remote_copy(
            src_ref=gated.at[source, block],
            dst_ref=gated.at[source, block],
            send_sem=gated_send.at[0],
            recv_sem=gated_recv.at[source, block],
            device_id={"chan": to},
            device_id_type=MESH,
        ).start()

    def arrived(source, block):
        slot = gated.at[source, block]
        pltpu.make_async_copy(slot, slot, gated_recv.at[source, block]).wait()

    def block_at(k):
        return lax.rem(x + blocks - BACK_ORDER[k], blocks)

    def gate(k):
        block = block_at(k)
        part = block_rows(block)
        pltpu.make_async_copy(conv_in.at[part], conv_in.at[part], conv_recv.at[block]).wait()
        value = conv_in[part, :].astype(jnp.float32).T
        gated[chan, block] = (value * query[block]).astype(jnp.bfloat16)
        for to in (far, down, sibling) if k == 0 else (down, sibling):
            pass_on(chan, block, to)

    def send_up(k):
        pass_on(chan, block_at(k), up)

    def near_up(k):
        block = block_at(k)
        arrived(up, block)
        if k > 0:
            pass_on(up, block, down)
        pass_on(up, block, sibling)

    def near_down(k):
        block = block_at(k)
        arrived(down, block)
        pass_on(down, block, sibling)

    def relay_far(k):
        block = block_at(k)
        arrived(far, block)
        pass_on(far, block, sibling)

    def project_part(k, sources):
        block = block_at(k)
        left = jnp.concatenate([gated[c, block] for c in sources], axis=1)
        right = jnp.concatenate(
            [
                weight[pl.ds(pl.multiple_of(c * channels + block * LANES, LANES), LANES), :]
                for c in sources
            ],
            axis=0,
        )
        return jnp.dot(left, right, preferred_element_type=jnp.float32)

    own_stream = (chan, up, down, far)
    other_stream = [c + 1 - 2 * core for c in own_stream]

    def project_mine(k):
        part = project_part(k, own_stream)
        if k == 0:
            out_total[...] = part
        else:
            out_total[...] += part

    def project_other(k):
        for c in other_stream:
            arrived(c, block_at(k))
        out_total[...] += project_part(k, other_stream)

    def project_near(k):
        for c in other_stream[:3]:
            arrived(c, block_at(k))
        out_total[...] += project_part(k, own_stream[:3] + tuple(other_stream[:3]))

    def project_rest(k):
        arrived(other_stream[3], block_at(k))
        part = project_part(k, (far, other_stream[3]))
        out_ref[...] = (out_total[...] + part).astype(jnp.bfloat16)

    load_weight.wait()
    steps = (
        (gate, 0), (send_up, 0), (gate, 1), (send_up, 1), (gate, 2),
        (send_up, 2), (gate, 3), (send_up, 3), (near_up, 0), (near_up, 1),
        (near_up, 2), (near_up, 3), (near_down, 0), (near_down, 1), (near_down, 2),
        (near_down, 3), (relay_far, 0), (relay_far, 1), (project_mine, 0), (project_other, 0),
        (relay_far, 2), (project_mine, 1), (project_other, 1), (project_mine, 2), (relay_far, 3),
        (project_other, 2), (project_near, 3), (project_rest, 3),
    )
    for step, k in steps:
        step(k)

    sent = product_out.at[0:2, pl.ds(0, (count - 1) * share), :]
    pltpu.make_async_copy(sent, sent, product_send.at[0]).wait()
    sent = conv_out.at[pl.ds(0, (count - 1) * share), :]
    pltpu.make_async_copy(sent, sent, conv_send.at[0]).wait()
    sent = filt_all.at[pl.ds(1, count - 1)]
    pltpu.make_async_copy(sent, sent, filt_sem.at[0]).wait()
    sent = gated.at[pl.ds(0, 7)]
    pltpu.make_async_copy(sent, sent, gated_send.at[0]).wait()


def solution(mesh):
    count = mesh.shape["seq"]
    chans = mesh.shape["chan"]
    planes, rings = 4, count // 4

    def per_device(projections, short_taps, filters, out_weight):
        rows, channels = projections.shape[1], projections.shape[2]
        blocks = channels // LANES
        share = channels // count
        vmem = pl.BlockSpec(memory_space=pltpu.VMEM)
        hbm = pl.BlockSpec(memory_space=pl.ANY)
        bf16, f32 = jnp.bfloat16, jnp.float32
        dma = pltpu.SemaphoreType.DMA
        return pl.pallas_call(
            functools.partial(kernel, (count, planes, rings)),
            out_shape=jax.ShapeDtypeStruct((rows, out_weight.shape[1]), bf16),
            in_specs=[hbm, hbm, hbm, hbm],
            out_specs=vmem,
            scratch_shapes=[
                pltpu.VMEM(short_taps.shape, f32),
                pltpu.VMEM(filters.shape, f32),
                pltpu.VMEM(projections.shape, bf16),
                pltpu.VMEM((PAD, channels), bf16),
                pltpu.VMEM((PAD, channels), bf16),
                pltpu.VMEM((PAD, channels), bf16),
                pltpu.VMEM((3, blocks, PAD + rows, LANES), f32),
                pltpu.VMEM((filters.shape[0], 1, rows), f32),
                pltpu.VMEM((count + 1, 1, rows), f32),
                pltpu.VMEM((count, LANES, rows), bf16),
                pltpu.VMEM((count, LANES, rows), bf16),
                pltpu.VMEM((blocks, LANES, LANES), f32),
                pltpu.VMEM((2, channels, LANES), bf16),
                pltpu.VMEM((2, LANES + channels, LANES), bf16),
                pltpu.VMEM((channels, rows), f32),
                pltpu.VMEM((channels, rows), bf16),
                pltpu.VMEM((channels, rows), bf16),
                pltpu.VMEM((blocks, rows, LANES), f32),
                pltpu.VMEM((chans, blocks, rows, LANES), bf16),
                pltpu.VMEM(out_weight.shape, bf16),
                pltpu.VMEM((rows, out_weight.shape[1]), f32),
                dma((5,)),
                dma((4,)),
                dma((2,)),
                dma((1,)),
                dma((blocks + 1,)),
                dma((1,)),
                dma((blocks,)),
                dma((1,)),
                dma((chans, blocks)),
            ],
            compiler_params=pltpu.CompilerParams(
                collective_id=0, has_side_effects=True, vmem_limit_bytes=24 * 2**20
            ),
        )(*[pltpu.with_memory_space_constraint(a, pltpu.HBM) for a in (projections, short_taps, filters, out_weight)])

    return jax.shard_map(
        per_device,
        mesh=mesh,
        in_specs=(P(None, "seq", "chan"), P(None, None, "chan"), P("chan", "seq"), P(None, "chan")),
        out_specs=P("seq", "chan"),
        check_vma=False,
    )
```

```python
import functools

import jax
import jax.numpy as jnp
from jax import lax
from jax.experimental import pallas as pl
from jax.experimental.pallas import tpu as pltpu
from jax.sharding import PartitionSpec as P

MESH = pl.DeviceIdType.MESH
TAPS = 7
EARLY_ORDER = (2, 3, 1, 0)
BACK_ORDER = (0, 2, 1, 3)
PAD = 16
LANES = 128


def kernel(
    sizes,
    proj_hbm,
    taps_hbm,
    filt_hbm,
    weight_hbm,
    out_ref,
    taps_ref,
    filt_ref,
    proj,
    halo,
    edge_out,
    edge_in,
    ext,
    filt_mine,
    filt_all,
    high,
    low,
    early,
    product_out,
    product_in,
    total,
    conv_out,
    conv_in,
    query,
    gated,
    weight,
    out_total,
    load_sem,
    halo_sem,
    filt_sem,
    product_send,
    product_recv,
    conv_send,
    conv_recv,
    gated_send,
    gated_recv,
):
    count, planes, rings = sizes
    rows = proj.shape[1]
    channels = proj.shape[2]
    share = channels // count
    blocks = channels // LANES
    per_block = count // blocks
    groups = filt_ref.shape[0]
    me = lax.axis_index("seq")
    chan = lax.axis_index("chan")
    x, z = me // rings, lax.rem(me, rings)
    y, core = chan // 2, lax.rem(chan, 2)
    heights = lax.axis_size("chan") // 2
    step_up = 1 - 2 * core
    down = lax.rem(y + step_up + heights, heights) * 2 + core
    up = lax.rem(y - step_up + heights, heights) * 2 + core
    far = lax.rem(y + 2, heights) * 2 + core
    sibling = y * 2 + 1 - core
    following = lax.rem(me + 1, count)
    mine = pl.ds(me * share, share)

    def ring_peer(dx, k):
        side = 1 - 2 * lax.rem(k, 2)
        dz = rings // 2 + side * ((k + 1) // 2)
        return lax.rem(x + dx, planes) * rings + lax.rem(z + dz, rings)

    def far_first(k):
        return ring_peer(lax.rem(k // rings + 2, planes), lax.rem(k, rings))

    def near_first(k):
        return ring_peer(k // rings, lax.rem(k, rings))

    def each_peer(order, skip, step):
        def one(k, carry):
            step(order(k))
            return carry

        lax.fori_loop(0, skip, one, 0)
        lax.fori_loop(skip + 1, count, one, 0)

    last_of = {far_first: 2 * rings + rings - 1, near_first: rings - 1}

    def to_all(order, step):
        each_peer(order, last_of[order], step)

    barrier = pltpu.get_barrier_semaphore()

    def greet(to):
        pl.semaphore_signal(barrier, inc=1, device_id={"seq": to}, device_id_type=MESH)

    to_all(far_first, greet)
    for other in (down, up, far, sibling):
        pl.semaphore_signal(barrier, inc=1, device_id={"chan": other}, device_id_type=MESH)

    load_taps = pltpu.make_async_copy(taps_hbm, taps_ref, load_sem.at[3])
    load_taps.start()
    load_filt = pltpu.make_async_copy(filt_hbm, filt_ref, load_sem.at[4])
    load_filt.start()
    load_pair = pltpu.make_async_copy(proj_hbm.at[1:3], proj.at[1:3], load_sem.at[0])
    load_pair.start()
    load_query = pltpu.make_async_copy(proj_hbm.at[0], proj.at[0], load_sem.at[1])
    load_query.start()
    load_weight = pltpu.make_async_copy(weight_hbm, weight, load_sem.at[2])

    for h in range(2):
        product_in[h, 0:LANES, :] = jnp.zeros((LANES, LANES), jnp.bfloat16)

    def widen(s):
        for q in range(blocks):
            ext[s, q, pl.ds(PAD, rows), :] = proj[s, :, q * LANES : (q + 1) * LANES].astype(jnp.float32)

    def short(s, q, first, size):
        lanes = pl.ds(pl.multiple_of(q * LANES, LANES), LANES)
        taps = taps_ref[s, :, lanes]
        value = taps[0:1, :] * ext[s, q, pl.ds(first + PAD, size), :]
        for j in range(1, TAPS):
            value = value + taps[j : j + 1, :] * ext[s, q, pl.ds(first + PAD - j, size), :]
        return value

    def each_block(step):
        def one(q, carry):
            step(q)
            return carry

        lax.fori_loop(0, blocks, one, 0)

    def block_rows(q):
        return pl.ds(pl.multiple_of(q * LANES, LANES), LANES)

    def late_products(q):
        value = short(1, q, LANES, LANES) * short(2, q, LANES, LANES)
        product_out[1, block_rows(q), :] = value.T.astype(jnp.bfloat16)

    def early_products(q):
        early[q, 8:, :] = short(1, q, 8, LANES - 8) * short(2, q, 8, LANES - 8)

    def send_product(h, to):
        pltpu.make_async_remote_copy(
            src_ref=product_out.at[h, pl.ds(to * share, share), :],
            dst_ref=product_in.at[h, pl.ds(LANES + me * share, share), :],
            send_sem=product_send.at[0],
            recv_sem=product_recv.at[blocks if h else x],
            device_id={"seq": to},
            device_id_type=MESH,
        ).start()

    def keep_product(h):
        pltpu.make_async_copy(
            product_out.at[h, mine, :],
            product_in.at[h, pl.ds(LANES + me * share, share), :],
            product_recv.at[blocks if h else x],
        ).start()

    load_taps.wait()
    load_pair.wait()
    widen(1)
    widen(2)
    each_block(late_products)

    load_filt.wait()
    for g in range(groups):
        filt_mine[g] = filt_ref[g : g + 1, :]
    filt_all[0] = jnp.zeros(filt_all.shape[1:], jnp.float32)
    for q in range(blocks):
        edge = [ext[s, q, pl.ds(PAD + rows - 8, 8), :] for s in (1, 2)]
        edge_out[:, q * LANES : (q + 1) * LANES] = jnp.concatenate(edge, axis=0).astype(jnp.bfloat16)

    pl.semaphore_wait(barrier, count + 3)

    def halo_of(source, target, at):
        return pltpu.make_async_remote_copy(
            src_ref=source,
            dst_ref=target,
            send_sem=halo_sem.at[at],
            recv_sem=halo_sem.at[at + 1],
            device_id={"seq": following},
            device_id_type=MESH,
        )

    pair_halo = halo_of(edge_out, edge_in, 0)
    pair_halo.start()

    def send_filter(to):
        pltpu.make_async_remote_copy(
            src_ref=filt_mine.at[to // (count // groups)],
            dst_ref=filt_all.at[me + 1],
            send_sem=filt_sem.at[0],
            recv_sem=filt_sem.at[1],
            device_id={"seq": to},
            device_id_type=MESH,
        ).start()

    to_all(far_first, send_filter)
    pltpu.make_async_copy(
        filt_mine.at[me // (count // groups)], filt_all.at[me + 1], filt_sem.at[1]
    ).start()
    to_all(far_first, functools.partial(send_product, 1))
    keep_product(1)

    each_block(early_products)
    pair_halo.wait()
    for q in range(blocks):
        edge = edge_in[:, q * LANES : (q + 1) * LANES].astype(jnp.float32)
        edge = jnp.where(me == 0, 0.0, edge)
        ext[1, q, 8:PAD, :] = edge[0:8]
        ext[2, q, 8:PAD, :] = edge[8:]

    def first_products(q):
        early[q, 0:8, :] = short(1, q, 0, 8) * short(2, q, 0, 8)
        product_out[0, block_rows(q), :] = early[q].T.astype(jnp.bfloat16)

    for dx in EARLY_ORDER:
        first_products(lax.rem(x + dx, planes))

        def one(i, carry):
            send_product(0, ring_peer(dx, i))
            return carry

        lax.fori_loop(0, rings - 1 if dx == 0 else rings, one, 0)
        if dx == 0:
            keep_product(0)
    load_weight.start()

    query_halo = halo_of(proj.at[0, pl.ds(rows - PAD, PAD), :], halo, 2)
    load_query.wait()
    query_halo.start()
    widen(0)
    def spread(d):
        line = jnp.concatenate([filt_all[d][:, rows - LANES :], filt_all[d + 1]], axis=1)
        wide = jnp.broadcast_to(line, (LANES, line.shape[1]))
        value = pltpu.roll(wide, 0, 1, stride=1, stride_axis=0)[:, LANES:]
        top = value.astype(jnp.bfloat16)
        high[d] = top
        low[d] = (value - top.astype(jnp.float32)).astype(jnp.bfloat16)

    def lagged(table, d):
        before = table[d - 1][:, LANES:] if d else jnp.zeros((LANES, LANES), jnp.bfloat16)
        return jnp.concatenate([before, table[d][:, :LANES]], axis=1)

    def convolve_late(d):
        size = channels - share * d
        left = jnp.concatenate(
            [
                product_in[1, LANES : LANES + size, :],
                product_in[1, LANES - share : LANES - share + size, :],
            ],
            axis=1,
        )
        part = None
        for table in (high, low):
            right = jnp.concatenate([lagged(table, d), lagged(table, d + 1)], axis=0)
            more = jnp.dot(left, right, preferred_element_type=jnp.float32)
            part = more if part is None else part + more
        if d == 0:
            total[...] = part
        else:
            total[share * d :, :] += part

    def early_arrived(dx):
        source = lax.rem(x + blocks - dx, blocks)
        place = product_in.at[0, pl.ds(pl.multiple_of((source + 1) * LANES, LANES), LANES), :]
        pltpu.make_async_copy(place, place, product_recv.at[source]).wait()

    def convolve_early(block, parts=None):
        base = pl.multiple_of(block * LANES, LANES)

        def lags(step, value):
            for e in range(0, per_block, 2):
                d = step * per_block + e
                first = LANES + base - share * d
                left = jnp.concatenate(
                    [
                        product_in[0, pl.ds(pl.multiple_of(first, share), LANES), :],
                        product_in[0, pl.ds(pl.multiple_of(first - share, share), LANES), :],
                    ],
                    axis=1,
                )
                for table in (high,):
                    right = table[pl.ds(d, 2)].reshape(2 * LANES, rows)
                    value = value + jnp.dot(left, right, preferred_element_type=jnp.float32)
            return value

        value = total[pl.ds(base, LANES), :]
        if parts is None:
            value = lax.fori_loop(0, block + 1, lags, value)
        else:
            for sources, steps in parts:
                for dx in sources:
                    early_arrived(dx)
                for step in steps:
                    stop = step + (block + blocks - step) // blocks
                    value = lax.fori_loop(step, stop, lags, value)
        conv_out[pl.ds(base, LANES), :] = value.astype(jnp.bfloat16)

    pltpu.make_async_copy(
        filt_all.at[pl.ds(1, count)], filt_all.at[pl.ds(1, count)], filt_sem.at[1]
    ).wait()
    for d in range(count):
        spread(d)
    whole = product_in.at[1, pl.ds(LANES, channels), :]
    pltpu.make_async_copy(whole, whole, product_recv.at[blocks]).wait()
    for d in range(0, count, 2):
        convolve_late(d)
    def send_back(to):
        pltpu.make_async_remote_copy(
            src_ref=conv_out.at[pl.ds(to * share, share), :],
            dst_ref=conv_in.at[mine, :],
            send_sem=conv_send.at[0],
            recv_sem=conv_recv.at[me // per_block],
            device_id={"seq": to},
            device_id_type=MESH,
        ).start()

    for dx in BACK_ORDER:
        if dx == 0:
            convolve_early(x, (((2, 3), (2, 3)), ((1,), (1,)), ((0,), (0,))))
        else:
            convolve_early(lax.rem(x + dx, blocks))

        def one(i, carry):
            send_back(ring_peer(dx, i))
            return carry

        lax.fori_loop(0, rings - 1 if dx == 0 else rings, one, 0)
        if dx == 0:
            own = conv_recv.at[me // per_block]
            pltpu.make_async_copy(conv_out.at[mine], conv_in.at[mine], own).start()

    def pass_on(source, block, to):
        pltpu.make_async_remote_copy(
            src_ref=gated.at[source, block],
            dst_ref=gated.at[source, block],
            send_sem=gated_send.at[0],
            recv_sem=gated_recv.at[source, block],
            device_id={"chan": to},
            device_id_type=MESH,
        ).start()

    def arrived(source, block):
        slot = gated.at[source, block]
        pltpu.make_async_copy(slot, slot, gated_recv.at[source, block]).wait()

    def block_at(k):
        return lax.rem(x + blocks - BACK_ORDER[k], blocks)

    def gate(k):
        block = block_at(k)
        part = block_rows(block)
        pltpu.make_async_copy(conv_in.at[part], conv_in.at[part], conv_recv.at[block]).wait()
        value = conv_in[part, :].astype(jnp.float32).T
        gated[chan, block] = (value * query[block]).astype(jnp.bfloat16)
        for to in (far, down, sibling) if k == 0 else (down, sibling):
            pass_on(chan, block, to)

    def send_up(k):
        pass_on(chan, block_at(k), up)

    def near_up(k):
        block = block_at(k)
        arrived(up, block)
        if k > 0:
            pass_on(up, block, down)
        pass_on(up, block, sibling)

    def near_down(k):
        block = block_at(k)
        arrived(down, block)
        pass_on(down, block, sibling)

    def relay_far(k):
        block = block_at(k)
        arrived(far, block)
        pass_on(far, block, sibling)

    def project_part(k, sources):
        block = block_at(k)
        left = jnp.concatenate([gated[c, block] for c in sources], axis=1)
        right = jnp.concatenate(
            [
                weight[pl.ds(pl.multiple_of(c * channels + block * LANES, LANES), LANES), :]
                for c in sources
            ],
            axis=0,
        )
        return jnp.dot(left, right, preferred_element_type=jnp.float32)

    own_stream = (chan, up, down, far)
    other_stream = [c + 1 - 2 * core for c in own_stream]

    def project_mine(k):
        part = project_part(k, own_stream)
        if k == 0:
            out_total[...] = part
        else:
            out_total[...] += part

    def project_other(k):
        for c in other_stream:
            arrived(c, block_at(k))
        out_total[...] += project_part(k, other_stream)

    def project_near(k):
        for c in other_stream[:3]:
            arrived(c, block_at(k))
        out_total[...] += project_part(k, own_stream[:3] + tuple(other_stream[:3]))

    def project_rest(k):
        arrived(other_stream[3], block_at(k))
        part = project_part(k, (far, other_stream[3]))
        out_ref[...] = (out_total[...] + part).astype(jnp.bfloat16)

    query_halo.wait()
    for q in range(blocks):
        before = halo[:, q * LANES : (q + 1) * LANES].astype(jnp.float32)
        ext[0, q, 0:PAD, :] = jnp.where(me == 0, 0.0, before)

    def queries(q):
        for first in (0, LANES):
            query[q, first : first + LANES, :] = short(0, q, first, LANES)

    each_block(queries)

    load_weight.wait()
    steps = (
        (gate, 0), (send_up, 0), (gate, 1), (send_up, 1), (gate, 2),
        (send_up, 2), (gate, 3), (send_up, 3), (near_up, 0), (near_up, 1),
        (near_up, 2), (near_up, 3), (near_down, 0), (near_down, 1), (near_down, 2),
        (near_down, 3), (relay_far, 0), (relay_far, 1), (project_mine, 0), (project_other, 0),
        (relay_far, 2), (project_mine, 1), (project_other, 1), (project_mine, 2), (relay_far, 3),
        (project_other, 2), (project_near, 3), (project_rest, 3),
    )
    for step, k in steps:
        step(k)

    sent = product_out.at[0:2, pl.ds(0, (count - 1) * share), :]
    pltpu.make_async_copy(sent, sent, product_send.at[0]).wait()
    sent = conv_out.at[pl.ds(0, (count - 1) * share), :]
    pltpu.make_async_copy(sent, sent, conv_send.at[0]).wait()
    sent = filt_all.at[pl.ds(1, count - 1)]
    pltpu.make_async_copy(sent, sent, filt_sem.at[0]).wait()
    sent = gated.at[pl.ds(0, 7)]
    pltpu.make_async_copy(sent, sent, gated_send.at[0]).wait()


def solution(mesh):
    count = mesh.shape["seq"]
    chans = mesh.shape["chan"]
    planes, rings = 4, count // 4

    def per_device(projections, short_taps, filters, out_weight):
        rows, channels = projections.shape[1], projections.shape[2]
        blocks = channels // LANES
        share = channels // count
        vmem = pl.BlockSpec(memory_space=pltpu.VMEM)
        hbm = pl.BlockSpec(memory_space=pl.ANY)
        bf16, f32 = jnp.bfloat16, jnp.float32
        dma = pltpu.SemaphoreType.DMA
        return pl.pallas_call(
            functools.partial(kernel, (count, planes, rings)),
            out_shape=jax.ShapeDtypeStruct((rows, out_weight.shape[1]), bf16),
            in_specs=[hbm, hbm, hbm, hbm],
            out_specs=vmem,
            scratch_shapes=[
                pltpu.VMEM(short_taps.shape, f32),
                pltpu.VMEM(filters.shape, f32),
                pltpu.VMEM(projections.shape, bf16),
                pltpu.VMEM((PAD, channels), bf16),
                pltpu.VMEM((PAD, channels), bf16),
                pltpu.VMEM((PAD, channels), bf16),
                pltpu.VMEM((3, blocks, PAD + rows, LANES), f32),
                pltpu.VMEM((filters.shape[0], 1, rows), f32),
                pltpu.VMEM((count + 1, 1, rows), f32),
                pltpu.VMEM((count, LANES, rows), bf16),
                pltpu.VMEM((count, LANES, rows), bf16),
                pltpu.VMEM((blocks, LANES, LANES), f32),
                pltpu.VMEM((2, channels, LANES), bf16),
                pltpu.VMEM((2, LANES + channels, LANES), bf16),
                pltpu.VMEM((channels, rows), f32),
                pltpu.VMEM((channels, rows), bf16),
                pltpu.VMEM((channels, rows), bf16),
                pltpu.VMEM((blocks, rows, LANES), f32),
                pltpu.VMEM((chans, blocks, rows, LANES), bf16),
                pltpu.VMEM(out_weight.shape, bf16),
                pltpu.VMEM((rows, out_weight.shape[1]), f32),
                dma((5,)),
                dma((4,)),
                dma((2,)),
                dma((1,)),
                dma((blocks + 1,)),
                dma((1,)),
                dma((blocks,)),
                dma((1,)),
                dma((chans, blocks)),
            ],
            compiler_params=pltpu.CompilerParams(
                collective_id=0, has_side_effects=True, vmem_limit_bytes=24 * 2**20
            ),
        )(*[pltpu.with_memory_space_constraint(a, pltpu.HBM) for a in (projections, short_taps, filters, out_weight)])

    return jax.shard_map(
        per_device,
        mesh=mesh,
        in_specs=(P(None, "seq", "chan"), P(None, None, "chan"), P("chan", "seq"), P(None, "chan")),
        out_specs=P("seq", "chan"),
        check_vma=False,
    )
```
